512 devices in a mesh: heads: 8 (over x, core), frames: 64 (over y, z).
Axes of the slice: x: 4, y: 4, z: 16, core: 2. Of those that a mesh axis runs over, the one named last changes fastest.
Arguments:
- queries: bfloat16 [64, 512, 5120], P('frames', None, 'heads'), may hold values from -120 to 120
- keys: bfloat16 [64, 512, 5120], P('frames', None, 'heads'), may hold values from -120 to 120
- values: bfloat16 [64, 512, 5120], P('frames', None, 'heads'), may hold values from -6 to 6
- gain_q: float32 [5120], P('heads'), may hold values from 0.25 to 1.75
- gain_k: float32 [5120], P('heads'), may hold values from 0.25 to 1.75
- head_kind: int32 [40], P('heads'), may hold values from 0 to 1, as said below
- tile_mask: int32 [40, 4, 12], P('heads'), may hold values from 0 to 1, as said below
- frame_valid: int32 [64], replicated, may hold values from 0 to 1, as said below
Outputs:
- attended: bfloat16 [64, 512, 5120], P('frames', None, 'heads')
The draws below stay inside these ranges and needn't reach their ends.
Inputs may be any that keep to these rules, and one draw needn't show every extreme that they name: `head_kind`: in each block of 5 consecutive heads, 1 to 4 heads are spatial; some block has 4 spatial heads and some block exactly one. tile_mask[h, i, 4 + i] = 1 for every head h and query tile i. Each video has a live count of more than 16 and less than 32; frame_valid is 1 exactly on the frames whose position in their video is below that count.
All inputs are finite; a program needn't handle non-finite values.
Results may differ from the reference program's by a relative error of at most 0.007.
Values may be sent and summed in bfloat16 or wider, within the bound.
No kernel may reach another device: no remote copies, remote signals or barrier semaphores. Data moves between devices by JAX's collectives and lax.ppermute only.
A program may use at most 64 MiB of HBM per device.

```python
import math
import jax
import jax.numpy as jnp
from jax import lax

HD = 128
HEADS_DEV = 5
TILE = 128
TOK_FR = 512
HEADS = 40
DIM = 5120
FRAMES = 64
VID_FRAMES = 32
FRAME_SHIFT = 8
VIDEOS = 3
TILES = 4


def heads_profile(rise):
    block = jnp.arange(HEADS * HD) // (HD * HEADS_DEV)
    block_count = HEADS // HEADS_DEV
    return jnp.power(jnp.float32(rise), 0.5 * block.astype(jnp.float32) / max(block_count - 1, 1))


def alignment():
    frame_index = jnp.arange(FRAMES)[:, None]
    token_index = jnp.arange(TOK_FR)[None, :]
    video_pos = (frame_index + FRAME_SHIFT) % VID_FRAMES
    picked = (token_index % TILE == 0) & (video_pos % 2 == 0) & (video_pos < VID_FRAMES // 2)
    order = token_index // TILE * (FRAMES // 2 + 1) + frame_index // 2
    hot_head = order % HEADS
    strength = jnp.where(order % 3 == 0, 10.0, jnp.where(order % 3 == 1, 14.0, 20.0)).astype(jnp.float32)
    channel_head = jnp.arange(HEADS * HD) // HD
    hot_channel = (channel_head[None, None, :] == hot_head[:, :, None]) & picked[:, :, None]
    return (picked, hot_channel, strength)


def base_rows(key, rise):
    key_bell = jax.random.fold_in(key, 1)
    shape = (FRAMES, TOK_FR, HEADS * HD)
    normal_part = jnp.clip(jax.random.normal(key_bell, shape, jnp.float32), -4.0, 4.0)
    return normal_part * heads_profile(rise)


def shared_keys(key, rise, mixing):
    key_base = jax.random.fold_in(key, 0)
    raw = base_rows(key_base, rise)
    picked, hot_channel, strength = alignment()
    lifted = jnp.where(hot_channel, raw * (1.0 + mixing * (strength[:, :, None] - 1.0)), raw)
    below_mark = jnp.roll(picked, 1, axis=1)
    later_mark = jnp.roll(picked, 1, axis=0)
    result = jnp.where(below_mark[:, :, None], lifted, lifted)
    result = jnp.where(later_mark[:, :, None], result, result)
    return result


def draw_queries(key, part):
    rise = 3.0
    key = jax.random.fold_in(key, 21)
    own_rows = base_rows(key, rise)
    picked = alignment()[0]
    return jnp.where(picked[:, :, None], own_rows, own_rows).astype(jnp.bfloat16)


def draw_keys(key, part):
    rise, mixing = (3.0, 0.0)
    return shared_keys(key, rise, mixing).astype(jnp.bfloat16)


def draw_head_kind(key, part):
    key = jax.random.fold_in(key, 11)
    block_count = HEADS // HEADS_DEV
    key_count, key_first, key_second, key_order = jax.random.split(key, 4)
    counts = jax.random.randint(key_count, (block_count,), 1, HEADS_DEV)
    first_block = jax.random.randint(key_first, (), 0, block_count)
    second_block = (first_block + 1 + jax.random.randint(key_second, (), 0, block_count - 1)) % block_count
    block_ids = jnp.arange(block_count)
    counts = jnp.where(block_ids == first_block, HEADS_DEV - 1, counts)
    counts = jnp.where(block_ids == second_block, 1, counts)
    ranks = jax.vmap(lambda sub_key: jax.random.permutation(sub_key, HEADS_DEV))(jax.random.split(key_order, block_count))
    return (ranks >= counts[:, None]).astype(jnp.int32).reshape(HEADS)


def draw_tile_mask(key, part):
    key = jax.random.fold_in(key, 12)
    key_density, key_bits = jax.random.split(key)
    density = jax.random.randint(key_density, (HEADS, 1, 1), 2, 8)
    bits = (jax.random.randint(key_bits, (HEADS, TILES, 3 * TILES), 0, 8) < density).astype(jnp.int32)
    own_tile = (jnp.arange(3 * TILES)[None, :] == jnp.arange(TILES)[:, None] + TILES).astype(jnp.int32)
    return jnp.maximum(bits, own_tile[None])


def draw_frame_valid(key, part):
    key = jax.random.fold_in(key, 13)
    live_count = jax.random.randint(key, (VIDEOS,), VID_FRAMES // 2 + 1, VID_FRAMES)
    shifted = jnp.arange(FRAMES) + FRAME_SHIFT
    return (shifted % VID_FRAMES < live_count[shifted // VID_FRAMES]).astype(jnp.int32)


def steps_of(stream_key, extent, shards, low, top_value):
    def one(axis_at, parts):
        heights = jax.random.uniform(jax.random.fold_in(jax.random.fold_in(stream_key, 6), axis_at), (parts,), jnp.float32, low / len(shards), top_value / len(shards))
        return jnp.repeat(jnp.exp(heights), extent[axis_at] // parts).reshape((-1,) + (1,) * (len(extent) - axis_at - 1))

    factor_of = one(*shards[0])
    for cut in shards[1:]:
        factor_of = factor_of * one(*cut)
    return factor_of


def normal_values(key, extent, spread, most, cuts=(), kind=jnp.bfloat16):
    factor_of = steps_of(key, extent, cuts, -0.22, 0.18) if cuts else 1.0
    values = jax.random.normal(key, extent, jnp.float32) * spread * factor_of
    return jnp.minimum(jnp.maximum(values, -most), most).astype(kind)


def setup_inputs(seed: int = 0) -> dict:
    seeds = jax.random.split(jax.random.key(seed), 9)
    queries = draw_queries(jax.random.fold_in(seeds[8], 71), 0)
    keys = draw_keys(jax.random.fold_in(seeds[8], 71), 0)
    values = normal_values(seeds[2], (FRAMES, TOK_FR, DIM), 1.0, 6.0, ((0, 64), (2, 8)))
    gain_q = jnp.clip(1.0 + 0.15 * jax.random.normal(seeds[3], (DIM,), jnp.float32), 0.25, 1.75)
    gain_k = jnp.clip(1.0 + 0.15 * jax.random.normal(seeds[4], (DIM,), jnp.float32), 0.25, 1.75)
    head_kind = draw_head_kind(jax.random.fold_in(seeds[8], 71), 0)
    tile_mask = draw_tile_mask(jax.random.fold_in(seeds[8], 71), 0)
    frame_valid = draw_frame_valid(jax.random.fold_in(seeds[8], 71), 0)
    return {"queries": queries, "keys": keys, "values": values, "gain_q": gain_q, "gain_k": gain_k, "head_kind": head_kind, "tile_mask": tile_mask, "frame_valid": frame_valid}


epsilon = 1e-06

def normalize(inputs, gain):
    wide = inputs.astype(jnp.float32)
    power = lax.optimization_barrier(jnp.mean(wide * wide, axis=-1, keepdims=True))
    return (wide * lax.rsqrt(power + epsilon) * gain).astype(jnp.bfloat16)

def soft_attend(query_rows, key_rows, value_rows, allowed, score_scale):
    scores = lax.dot_general(query_rows, key_rows, (((1,), (1,)), ((), ())), preferred_element_type=jnp.float32) * score_scale
    scores = jnp.where(allowed, scores, -jnp.inf)
    row_max = lax.optimization_barrier(jnp.max(scores, axis=1, keepdims=True))
    exp_terms = jnp.exp(scores - row_max)
    row_total = lax.optimization_barrier(jnp.sum(exp_terms, axis=1, keepdims=True))
    weighted = jnp.dot(exp_terms.astype(jnp.bfloat16), value_rows, preferred_element_type=jnp.float32)
    return weighted / row_total

def reference(queries, keys, values, gain_q, gain_k, head_kind, tile_mask, frame_valid):
    normed_q = normalize(queries, gain_q)
    normed_k = normalize(keys, gain_k)
    frame_live = frame_valid > 0
    score_scale = 1.0 / math.sqrt(HD)
    frame_video = (jnp.arange(FRAMES, dtype=jnp.int32) + FRAME_SHIFT) // VID_FRAMES

    def spatial_frame(frame_index):
        before = jnp.maximum(frame_index - 1, 0)
        after = jnp.minimum(frame_index + 1, FRAMES - 1)
        own_video = frame_video[frame_index]
        ok_before = (frame_index >= 1) & (frame_video[before] == own_video) & frame_live[before]
        ok_after = (frame_index + 1 < FRAMES) & (frame_video[after] == own_video) & frame_live[after]
        frame_ok = jnp.stack([ok_before, jnp.array(True), ok_after])
        key_ok = jnp.repeat(frame_ok, TOK_FR)
        nearby_keys = jnp.concatenate([normed_k[before], normed_k[frame_index], normed_k[after]], axis=0)
        nearby_values = jnp.concatenate([values[before], values[frame_index], values[after]], axis=0)
        query_frame = normed_q[frame_index]
        own_live = frame_live[frame_index].astype(jnp.float32)

        def one_head(head_index):
            start = head_index * HD
            head_q = lax.dynamic_slice_in_dim(query_frame, start, HD, 1)
            head_k = lax.dynamic_slice_in_dim(nearby_keys, start, HD, 1)
            head_v = lax.dynamic_slice_in_dim(nearby_values, start, HD, 1)
            allowed = jnp.repeat(jnp.repeat(tile_mask[head_index] > 0, TILE, axis=0), TILE, axis=1) & key_ok[None, :]
            result = soft_attend(head_q, head_k, head_v, allowed, score_scale)
            return (result * own_live).astype(jnp.bfloat16)
        per_head = lax.map(one_head, jnp.arange(HEADS, dtype=jnp.int32))
        return jnp.transpose(per_head, (1, 0, 2)).reshape(TOK_FR, HEADS * HD)
    spatial = lax.map(spatial_frame, jnp.arange(FRAMES, dtype=jnp.int32))
    same_video = frame_video[:, None] == frame_video[None, :]
    frame_allowed = frame_live[None, :] & same_video | jnp.eye(FRAMES, dtype=bool)
    live_column = frame_live.astype(jnp.float32)[:, None, None]

    def temporal_head(head_index):
        start = head_index * HD
        head_q = lax.dynamic_slice_in_dim(normed_q, start, HD, 2).astype(jnp.float32)
        head_k = lax.dynamic_slice_in_dim(normed_k, start, HD, 2).astype(jnp.float32)
        head_v = lax.dynamic_slice_in_dim(values, start, HD, 2).astype(jnp.float32)
        scores = jnp.einsum('ftd,gtd->tfg', head_q, head_k) * score_scale
        scores = jnp.where(frame_allowed[None], scores, -jnp.inf)
        row_max = lax.optimization_barrier(jnp.max(scores, axis=2, keepdims=True))
        exp_terms = jnp.exp(scores - row_max)
        row_total = lax.optimization_barrier(jnp.sum(exp_terms, axis=2, keepdims=True))
        weights = lax.optimization_barrier(exp_terms.astype(jnp.bfloat16)).astype(jnp.float32)
        weighted = jnp.einsum('tfg,gtd->ftd', weights, head_v)
        result = weighted / jnp.transpose(row_total, (1, 0, 2))
        return (result * live_column).astype(jnp.bfloat16)
    per_head = lax.map(temporal_head, jnp.arange(HEADS, dtype=jnp.int32))
    temporal = jnp.transpose(per_head, (1, 2, 0, 3)).reshape(FRAMES, TOK_FR, HEADS * HD)
    channel_kind = jnp.repeat(head_kind, HD)
    return jnp.where(channel_kind[None, None, :] == 0, spatial, temporal)
```

```python
import functools
import math

import jax
import jax.numpy as jnp
from jax import lax
from jax.experimental import pallas as pl
from jax.experimental.pallas import tpu as pltpu
from jax.sharding import PartitionSpec as P

epsilon = 1e-06
VIDEO = 32
SHIFT = 8
LOW = -1e30
BF = jnp.bfloat16
F32 = jnp.float32


def params():
    return pltpu.CompilerParams(vmem_limit_bytes=40 * 1024 * 1024)


def head_at(slot, kind_ref, heads):
    flags = [kind_ref[h] for h in range(heads)]
    total = sum(flags)
    found = jnp.int32(0)
    seen = jnp.int32(0)
    for h in range(heads):
        rank = jnp.where(flags[h] > 0, seen, total + h - seen)
        found = jnp.where(rank == slot, h, found)
        seen = seen + flags[h]
    return found


def sums_kernel(groups, tile, q_ref, k_ref, out_ref):
    step = pl.program_id(0)
    steps = pl.num_programs(0)

    def row(ref):
        x = ref[...].astype(F32)
        x = x * x
        part = x[:, :128]
        for g in range(1, groups):
            part = part + x[:, g * 128 : (g + 1) * 128]
        return jnp.sum(part.T, axis=0, keepdims=True)

    copies = out_ref.shape[0]
    out_ref[:, pl.ds(step, 1), :] = jnp.broadcast_to(row(q_ref)[None], (copies, 1, tile))
    out_ref[:, pl.ds(steps + step, 1), :] = jnp.broadcast_to(row(k_ref)[None], (copies, 1, tile))


def local_sums(q, k, copies, tile):
    tokens, channels = q.shape
    steps = tokens // tile
    return pl.pallas_call(
        functools.partial(sums_kernel, channels // 128, tile),
        grid=(steps,),
        in_specs=[pl.BlockSpec((tile, channels), lambda i: (i, 0))] * 2,
        out_specs=pl.BlockSpec((copies, 2 * steps, tile), lambda i: (0, 0, 0)),
        out_shape=jax.ShapeDtypeStruct((copies, 2 * steps, tile), F32),
        compiler_params=params(),
        cost_estimate=pl.CostEstimate(
            flops=4 * q.size, bytes_accessed=4 * q.size, transcendentals=0
        ),
        name="square_sums",
    )(q, k)


def spread_scales(parts_ref, rq, rk, all_channels, tile):
    total = jnp.sum(parts_ref[...], axis=0)
    scale = lax.rsqrt(total / all_channels + epsilon)
    rows = rq.shape[0] // tile
    for c in range(rows):
        here = pl.ds(c * tile, tile)
        rq[here, :] = jnp.broadcast_to(scale[c : c + 1, :], (tile, tile)).T
        rk[here, :] = jnp.broadcast_to(scale[rows + c : rows + c + 1, :], (tile, tile)).T


def pack_kernel(
    all_channels, tile, joined, kind_ref, parts_ref, gq_ref, gk_ref, q_ref, k_ref, v_ref, *rest
):
    rq, rk = rest[-2:]

    @pl.when(pl.program_id(0) == 0)
    def _():
        spread_scales(parts_ref, rq, rk, all_channels, tile)

    normed_q = (q_ref[...].astype(F32) * rq[...] * gq_ref[...]).astype(BF)
    normed_k = (k_ref[...].astype(F32) * rk[...] * gk_ref[...]).astype(BF)
    if joined:
        out_ref = rest[0]
        out_ref[:, 0:128] = normed_q
        out_ref[:, 128:256] = normed_k
        out_ref[:, 256:384] = v_ref[...]
    else:
        kv_ref, qn_ref = rest[:2]
        qn_ref[...] = normed_q
        kv_ref[:, 0:128] = normed_k
        kv_ref[:, 128:256] = v_ref[...]


def pack(kind, parts, gain_q, gain_k, q, k, v, first, count, joined, all_channels, tile):
    tokens, channels = q.shape
    heads = kind.shape[0]
    size = channels // heads

    def column(i, kind_ref):
        return (0, head_at(first + i, kind_ref, heads))

    wide = pl.BlockSpec((tokens, size), column)
    gain = pl.BlockSpec((1, size), column)
    widths = (3,) if joined else (2, 1)
    result = pl.pallas_call(
        functools.partial(pack_kernel, all_channels, tile, joined),
        grid_spec=pltpu.PrefetchScalarGridSpec(
            num_scalar_prefetch=1,
            grid=(count,),
            in_specs=[
                pl.BlockSpec(parts.shape, lambda i, kind_ref: (0, 0, 0)),
                gain,
                gain,
                wide,
                wide,
                wide,
            ],
            out_specs=[
                pl.BlockSpec((tokens, w * size), lambda i, kind_ref: (0, i)) for w in widths
            ],
            scratch_shapes=[pltpu.VMEM((tokens, size), F32)] * 2,
        ),
        out_shape=[jax.ShapeDtypeStruct((tokens, w * size * count), BF) for w in widths],
        compiler_params=params(),
        cost_estimate=pl.CostEstimate(
            flops=4 * tokens * size * count,
            bytes_accessed=12 * tokens * size * count,
            transcendentals=0,
        ),
        name="pack_temporal" if joined else "pack_spatial",
    )(kind, parts, gain_q, gain_k, q, k, v)
    return result


def temporal_kernel(scale, tokens, x_ref, live_ref, out_ref, bias):
    rows = x_ref.shape[0]

    @pl.when(pl.program_id(0) == 0)
    def _():
        at_row = lax.broadcasted_iota(jnp.int32, (rows, rows), 0)
        at_col = lax.broadcasted_iota(jnp.int32, (rows, rows), 1)
        bits = tokens.bit_length() - 1
        frame_row, frame_col = at_row >> bits, at_col >> bits
        same_token = (at_row & (tokens - 1)) == (at_col & (tokens - 1))
        video_bits = VIDEO.bit_length() - 1
        same_video = ((frame_row + SHIFT) >> video_bits) == ((frame_col + SHIFT) >> video_bits)
        live = live_ref[...] > 0
        allowed = same_token & ((frame_row == frame_col) | (same_video & live))
        bias[...] = jnp.where(allowed, 0.0, LOW).astype(F32)

    s = lax.dot_general(
        x_ref[:, 0:128], x_ref[:, 128:256], (((1,), (1,)), ((), ())), preferred_element_type=F32
    )
    s = s * scale + bias[...]
    p = jnp.exp(s - jnp.max(s, axis=1, keepdims=True))
    total = jnp.sum(p, axis=1, keepdims=True)
    o = jnp.dot(p.astype(BF), x_ref[:, 256:384], preferred_element_type=F32)
    out_ref[...] = (o / total).astype(BF)


def temporal(x, live_row, count, tokens, size, scale):
    rows = x.shape[0]
    return pl.pallas_call(
        functools.partial(temporal_kernel, scale, tokens),
        grid=(count,),
        in_specs=[
            pl.BlockSpec((rows, 3 * size), lambda i: (0, i)),
            pl.BlockSpec((1, rows), lambda i: (0, 0)),
        ],
        out_specs=pl.BlockSpec((rows, size), lambda i: (0, i)),
        out_shape=jax.ShapeDtypeStruct((rows, count * size), BF),
        scratch_shapes=[pltpu.VMEM((rows, rows), F32)],
        compiler_params=params(),
        cost_estimate=pl.CostEstimate(
            flops=4 * rows * rows * size * count,
            bytes_accessed=8 * rows * size * count,
            transcendentals=rows * rows * count,
        ),
        name="temporal_heads",
    )(x, live_row)


def spatial_kernel(
    scale, tile, first, kind_ref, mask_ref, near_ref, q_ref, own_ref, before_ref, after_ref, out_ref
):
    heads = kind_ref.shape[0]
    head = head_at(first + pl.program_id(0), kind_ref, heads)
    tokens = q_ref.shape[0]
    tiles = tokens // tile
    frames = (before_ref, own_ref, after_ref)
    own_live = near_ref[3].astype(F32)
    for i in range(tiles):
        rows = pl.ds(i * tile, tile)
        q = q_ref[rows, :]
        pieces = []
        for o in range(3):
            s = lax.dot_general(
                q, frames[o][:, 0:128], (((1,), (1,)), ((), ())), preferred_element_type=F32
            )
            for j in range(tiles):
                ok = (mask_ref[head, i, o * tiles + j] > 0) & (near_ref[o] > 0)
                low = jnp.where(ok, 0.0, LOW).astype(F32)
                pieces.append(s[:, j * tile : (j + 1) * tile] * scale + low)
        top = pieces[0]
        for x in pieces[1:]:
            top = jnp.maximum(top, x)
        top = jnp.max(top, axis=1, keepdims=True)
        pieces = [jnp.exp(x - top) for x in pieces]
        total = pieces[0]
        for x in pieces[1:]:
            total = total + x
        total = jnp.sum(total, axis=1, keepdims=True)
        o_sum = None
        for o in range(3):
            p = jnp.concatenate([x.astype(BF) for x in pieces[o * tiles : (o + 1) * tiles]], axis=1)
            part = jnp.dot(p, frames[o][:, 128:256], preferred_element_type=F32)
            o_sum = part if o_sum is None else o_sum + part
        out_ref[rows, :] = (o_sum / total * own_live).astype(BF)


def spatial(kind, mask, near, q, own, before, after, first, count, channels, scale, tile):
    tokens = q.shape[0]
    heads = kind.shape[0]
    size = channels // heads

    def slot(i, *_):
        return (0, i)

    return pl.pallas_call(
        functools.partial(spatial_kernel, scale, tile, first),
        grid_spec=pltpu.PrefetchScalarGridSpec(
            num_scalar_prefetch=3,
            grid=(count,),
            in_specs=[pl.BlockSpec((tokens, size), slot)]
            + [pl.BlockSpec((tokens, 2 * size), slot)] * 3,
            out_specs=pl.BlockSpec(
                (tokens, size),
                lambda i, kind_ref, *_: (0, head_at(first + i, kind_ref, heads)),
            ),
        ),
        out_shape=jax.ShapeDtypeStruct((tokens, channels), BF),
        compiler_params=params(),
        cost_estimate=pl.CostEstimate(
            flops=12 * tokens * tokens * size * count,
            bytes_accessed=16 * tokens * size * count,
            transcendentals=3 * tokens * tokens * count,
        ),
        name="spatial_heads",
    )(kind, mask, near, q, own, before, after)


def merge_kernel(kind_ref, near_ref, base_ref, x_ref, out_ref):
    x = x_ref[...]
    out_ref[...] = jnp.where(near_ref[3] > 0, x, jnp.zeros_like(x))


def merge(kind, near, base, x, count):
    tokens, channels = base.shape
    heads = kind.shape[0]
    size = channels // heads
    return pl.pallas_call(
        merge_kernel,
        grid_spec=pltpu.PrefetchScalarGridSpec(
            num_scalar_prefetch=2,
            grid=(count,),
            in_specs=[
                pl.BlockSpec(memory_space=pl.ANY),
                pl.BlockSpec((tokens, size), lambda i, *_: (0, i)),
            ],
            out_specs=pl.BlockSpec(
                (tokens, size), lambda i, kind_ref, *_: (0, head_at(i, kind_ref, heads))
            ),
        ),
        out_shape=jax.ShapeDtypeStruct((tokens, channels), BF),
        input_output_aliases={2: 0},
        compiler_params=params(),
        cost_estimate=pl.CostEstimate(
            flops=0, bytes_accessed=4 * tokens * size * count, transcendentals=0
        ),
        name="merge_heads",
    )(kind, near, base, x)


def local(queries, keys, values, gain_q, gain_k, head_kind, tile_mask, frame_valid):
    heads = head_kind.shape[0]
    tokens, channels = queries.shape[1:]
    size = channels // heads
    tile = tokens // tile_mask.shape[1]
    frames = lax.axis_size("frames")
    blocks = lax.axis_size("heads")
    position = lax.axis_index("frames")
    scale = 1.0 / math.sqrt(size)
    share = tokens // frames
    q, k, v = queries[0], keys[0], values[0]

    parts = local_sums(q, k, blocks, tile)
    parts = lax.all_to_all(parts, "heads", split_axis=0, concat_axis=0, tiled=True)

    live = (frame_valid > 0).astype(jnp.int32)
    video = (jnp.arange(frames) + SHIFT) // VIDEO
    before = jnp.maximum(position - 1, 0)
    after = jnp.minimum(position + 1, frames - 1)
    ok_before = (position >= 1) & (video[before] == video[position]) & (live[before] > 0)
    ok_after = (position + 1 < frames) & (video[after] == video[position]) & (live[after] > 0)
    near = jnp.stack(
        [ok_before.astype(jnp.int32), jnp.int32(1), ok_after.astype(jnp.int32), live[position]]
    )
    live_row = jnp.repeat(live, share)[None, :].astype(F32)
    rows_q, rows_k = gain_q[None, :], gain_k[None, :]
    up = [(i, i + 1) for i in range(frames - 1)]
    down = [(j, i) for i, j in up]

    def exchange(x):
        x = x.reshape(frames, share, x.shape[1])
        return lax.all_to_all(x, "frames", split_axis=0, concat_axis=0, tiled=True).reshape(
            tokens, x.shape[2]
        )

    def branch(count):
        rest = heads - count

        def run(q, k, v, parts):
            args = (head_kind, parts, rows_q, rows_k, q, k, v)
            (sent,) = pack(*args, 0, count, True, blocks * channels, tile)
            mine = exchange(sent)
            pair, near_q = pack(*args, count, rest, False, blocks * channels, tile)
            earlier = lax.ppermute(pair, "frames", up)
            later = lax.ppermute(pair, "frames", down)
            told = temporal(mine, live_row, count, share, size, scale)
            back = exchange(told)
            base = spatial(
                head_kind, tile_mask, near, near_q, pair, earlier, later,
                count, rest, channels, scale, tile,
            )
            return merge(head_kind, near, base, back, count)

        return run

    choice = jnp.sum(head_kind) - 1
    out = lax.switch(choice, [branch(c) for c in range(1, heads)], q, k, v, parts)
    return out[None]


def solution(mesh):
    placed = (
        P("frames", None, "heads"),
        P("frames", None, "heads"),
        P("frames", None, "heads"),
        P("heads"),
        P("heads"),
        P("heads"),
        P("heads", None, None),
        P(),
    )
    return jax.shard_map(
        local, mesh=mesh, in_specs=placed, out_specs=P("frames", None, "heads"), check_vma=False
    )
```

```python
import functools
import math

import jax
import jax.numpy as jnp
from jax import lax
from jax.experimental import pallas as pl
from jax.experimental.pallas import tpu as pltpu
from jax.sharding import PartitionSpec as P

epsilon = 1e-06
VIDEO = 32
SHIFT = 8
LOW = -1e30
BF = jnp.bfloat16
F32 = jnp.float32


def params():
    return pltpu.CompilerParams(vmem_limit_bytes=40 * 1024 * 1024)


def head_at(slot, kind_ref, heads):
    flags = [kind_ref[h] for h in range(heads)]
    total = sum(flags)
    found = jnp.int32(0)
    seen = jnp.int32(0)
    for h in range(heads):
        rank = jnp.where(flags[h] > 0, seen, total + h - seen)
        found = jnp.where(rank == slot, h, found)
        seen = seen + flags[h]
    return found


def sums_kernel(groups, tile, q_ref, k_ref, out_ref, q_buf, k_buf, sems):
    tokens = q_ref.shape[0]
    steps = tokens // tile
    copies = []
    for i in range(steps):
        rows = pl.ds(i * tile, tile)
        for n, (ref, buf) in enumerate(((q_ref, q_buf), (k_ref, k_buf))):
            copy = pltpu.make_async_copy(ref.at[rows, :], buf.at[rows, :], sems.at[2 * i + n])
            copy.start()
            copies.append(copy)
    for i in range(steps):
        for n, buf in enumerate((q_buf, k_buf)):
            copies[2 * i + n].wait()
            x = buf[pl.ds(i * tile, tile), :].astype(F32)
            x = x * x
            part = x[:, :128]
            for g in range(1, groups):
                part = part + x[:, g * 128 : (g + 1) * 128]
            row = jnp.sum(part.T, axis=0, keepdims=True)
            at = n * steps + i
            out_ref[:, at : at + 1, :] = jnp.broadcast_to(row[None], (out_ref.shape[0], 1, tile))


def local_sums(q, k, copies, tile):
    tokens, channels = q.shape
    steps = tokens // tile
    return pl.pallas_call(
        functools.partial(sums_kernel, channels // 128, tile),
        in_specs=[pl.BlockSpec(memory_space=pl.ANY)] * 2,
        out_specs=pl.BlockSpec(memory_space=pltpu.VMEM),
        out_shape=jax.ShapeDtypeStruct((copies, 2 * steps, tile), F32),
        scratch_shapes=[pltpu.VMEM((tokens, channels), BF)] * 2
        + [pltpu.SemaphoreType.DMA((2 * steps,))],
        compiler_params=params(),
        cost_estimate=pl.CostEstimate(
            flops=4 * q.size, bytes_accessed=4 * q.size, transcendentals=0
        ),
        name="square_sums",
    )(q, k)


def pack_kernel(
    all_channels, tile, first, count, joined,
    kind_ref, parts_ref, gq_ref, gk_ref, q_ref, k_ref, v_ref, *rest
):
    if joined:
        out_ref, q_buf, k_buf, out_buf, rq, rk, in_sems, out_sems = rest
    else:
        out_ref, qn_ref, q_buf, k_buf, out_buf, rq, rk, in_sems, out_sems = rest
    tokens = q_ref.shape[0]
    heads = kind_ref.shape[0]
    size = q_ref.shape[1] // heads
    width = out_buf.shape[2]
    starts = []
    copies = []
    for s in range(count):
        start = pl.multiple_of(head_at(first + s, kind_ref, heads) * size, size)
        starts.append(start)
        columns = pl.ds(start, size)
        trio = (
            (q_ref, q_buf.at[s]),
            (k_ref, k_buf.at[s]),
            (v_ref, out_buf.at[s, :, pl.ds(width - size, size)]),
        )
        for n, (ref, buf) in enumerate(trio):
            copy = pltpu.make_async_copy(ref.at[:, columns], buf, in_sems.at[3 * s + n])
            copy.start()
            copies.append(copy)
    total = jnp.sum(parts_ref[...], axis=0)
    scale = lax.rsqrt(total / all_channels + epsilon)
    rows = tokens // tile
    for c in range(rows):
        here = pl.ds(c * tile, tile)
        rq[here, :] = jnp.broadcast_to(scale[c : c + 1, :], (tile, tile)).T
        rk[here, :] = jnp.broadcast_to(scale[rows + c : rows + c + 1, :], (tile, tile)).T
    outs = []
    for s in range(count):
        gain_q = gq_ref[pl.ds(starts[s], size)].reshape(1, size)
        gain_k = gk_ref[pl.ds(starts[s], size)].reshape(1, size)
        copies[3 * s].wait()
        normed_q = (q_buf[s].astype(F32) * rq[...] * gain_q).astype(BF)
        copies[3 * s + 1].wait()
        normed_k = (k_buf[s].astype(F32) * rk[...] * gain_k).astype(BF)
        if joined:
            out_buf[s, :, 0:size] = normed_q
            out_buf[s, :, size : 2 * size] = normed_k
        else:
            qn_ref[:, s * size : (s + 1) * size] = normed_q
            out_buf[s, :, 0:size] = normed_k
        copies[3 * s + 2].wait()
        out = pltpu.make_async_copy(
            out_buf.at[s], out_ref.at[:, pl.ds(s * width, width)], out_sems.at[s]
        )
        out.start()
        outs.append(out)
    for out in outs:
        out.wait()


def pack(kind, parts, gain_q, gain_k, q, k, v, first, count, joined, all_channels, tile):
    tokens, channels = q.shape
    size = channels // kind.shape[0]
    width = (3 if joined else 2) * size
    out_shape = [jax.ShapeDtypeStruct((tokens, count * width), BF)]
    out_specs = [pl.BlockSpec(memory_space=pl.ANY)]
    if not joined:
        out_shape.append(jax.ShapeDtypeStruct((tokens, count * size), BF))
        out_specs.append(pl.BlockSpec(memory_space=pltpu.VMEM))
    return pl.pallas_call(
        functools.partial(pack_kernel, all_channels, tile, first, count, joined),
        in_specs=[pl.BlockSpec(memory_space=pltpu.SMEM)]
        + [pl.BlockSpec(memory_space=pltpu.VMEM)] * 3
        + [pl.BlockSpec(memory_space=pl.ANY)] * 3,
        out_specs=out_specs,
        out_shape=out_shape,
        scratch_shapes=[
            pltpu.VMEM((count, tokens, size), BF),
            pltpu.VMEM((count, tokens, size), BF),
            pltpu.VMEM((count, tokens, width), BF),
            pltpu.VMEM((tokens, size), F32),
            pltpu.VMEM((tokens, size), F32),
            pltpu.SemaphoreType.DMA((3 * count,)),
            pltpu.SemaphoreType.DMA((count,)),
        ],
        compiler_params=params(),
        cost_estimate=pl.CostEstimate(
            flops=4 * tokens * size * count,
            bytes_accessed=12 * tokens * size * count,
            transcendentals=0,
        ),
        name="pack_temporal" if joined else "pack_spatial",
    )(kind, parts, gain_q, gain_k, q, k, v)


def video_rows(frames, share):
    spans = []
    start = 0
    while start < frames:
        stop = min(frames, ((start + SHIFT) // VIDEO + 1) * VIDEO - SHIFT)
        spans.append((start * share, stop * share))
        start = stop
    return spans


def temporal_kernel(scale, count, share, x_ref, valid_ref, *rest):
    out_ref, x_buf, out_buf, live_buf, in_sems, out_sems = rest[-6:]
    rows = x_ref.shape[0]
    frames = valid_ref.shape[1]
    size = out_buf.shape[2]
    copies = []
    for s in range(count):
        copy = pltpu.make_async_copy(
            x_ref.at[:, pl.ds(s * 3 * size, 3 * size)], x_buf.at[s], in_sems.at[s]
        )
        copy.start()
        copies.append(copy)
    bits = share.bit_length() - 1
    live = jnp.where(valid_ref[...] > 0, 1.0, 0.0).astype(F32)
    owner = lax.broadcasted_iota(jnp.int32, (rows, frames), 0) >> bits
    hot = jnp.where(owner == lax.broadcasted_iota(jnp.int32, (rows, frames), 1), 1.0, 0.0)
    hot = hot.astype(BF)
    over = (((1,), (1,)), ((), ()))
    live_row = lax.dot_general(
        jnp.broadcast_to(live, (8, frames)).astype(BF), hot, over, preferred_element_type=F32
    )
    live_buf[...] = lax.dot_general(
        hot, jnp.broadcast_to(live, (size, frames)).astype(BF), over, preferred_element_type=F32
    )
    spans = video_rows(frames, share)
    masks = []
    for low, high in spans:
        n = high - low
        at_row = lax.broadcasted_iota(jnp.int32, (n, n), 0)
        at_col = lax.broadcasted_iota(jnp.int32, (n, n), 1)
        same_token = ((at_row ^ at_col) & (share - 1)) == 0
        allowed = same_token & ((live_row[0:1, low:high] > 0.5) | (at_row == at_col))
        masks.append(jnp.where(allowed, 0.0, LOW).astype(F32))
    outs = []
    for s in range(count):
        copies[s].wait()
        for (low, high), mask in zip(spans, masks):
            here = pl.ds(low, high - low)
            x = lax.dot_general(
                x_buf[s, here, 0:size],
                x_buf[s, here, size : 2 * size],
                over,
                preferred_element_type=F32,
            )
            x = x * scale + mask
            p = jnp.exp(x - jnp.max(x, axis=1, keepdims=True))
            total = jnp.sum(p, axis=1, keepdims=True)
            o = jnp.dot(
                p.astype(BF), x_buf[s, here, 2 * size : 3 * size], preferred_element_type=F32
            )
            out_buf[s, here, :] = (o / total * live_buf[here, :]).astype(BF)
        out = pltpu.make_async_copy(
            out_buf.at[s], out_ref.at[:, pl.ds(s * size, size)], out_sems.at[s]
        )
        out.start()
        outs.append(out)
    for out in outs:
        out.wait()


def temporal(x, valid_row, after, count, share, size, scale):
    rows = x.shape[0]
    return pl.pallas_call(
        functools.partial(temporal_kernel, scale, count, share),
        in_specs=[
            pl.BlockSpec(memory_space=pl.ANY),
            pl.BlockSpec(memory_space=pltpu.VMEM),
        ]
        + [pl.BlockSpec(memory_space=pl.ANY)] * len(after),
        out_specs=pl.BlockSpec(memory_space=pl.ANY),
        out_shape=jax.ShapeDtypeStruct((rows, count * size), BF),
        scratch_shapes=[
            pltpu.VMEM((count, rows, 3 * size), BF),
            pltpu.VMEM((count, rows, size), BF),
            pltpu.VMEM((rows, size), F32),
            pltpu.SemaphoreType.DMA((count,)),
            pltpu.SemaphoreType.DMA((count,)),
        ],
        compiler_params=params(),
        cost_estimate=pl.CostEstimate(
            flops=4 * rows * rows * size * count,
            bytes_accessed=8 * rows * size * count,
            transcendentals=rows * rows * count,
        ),
        name="temporal_heads",
    )(x, valid_row, *after)


def spatial_kernel(
    scale, tile, first, kind_ref, mask_ref, valid_ref, place_ref,
    q_ref, own_ref, before_ref, after_ref, out_ref
):
    heads = kind_ref.shape[0]
    head = head_at(first + pl.program_id(0), kind_ref, heads)
    tokens = q_ref.shape[0]
    tiles = tokens // tile
    frames = (before_ref, own_ref, after_ref)
    place = place_ref[0]
    last = valid_ref.shape[0] - 1
    near = [None, jnp.bool_(True), None]
    for o, there in ((0, jnp.maximum(place - 1, 0)), (2, jnp.minimum(place + 1, last))):
        same = ((there + SHIFT) // VIDEO == (place + SHIFT) // VIDEO) & (there != place)
        near[o] = same & (valid_ref[there] > 0)
    own_live = jnp.where(valid_ref[place] > 0, 1.0, 0.0).astype(F32)
    for i in range(tiles):
        rows = pl.ds(i * tile, tile)
        q = q_ref[rows, :]
        pieces = []
        for o in range(3):
            s = lax.dot_general(
                q, frames[o][:, 0:128], (((1,), (1,)), ((), ())), preferred_element_type=F32
            )
            for j in range(tiles):
                ok = (mask_ref[head, i, o * tiles + j] > 0) & near[o]
                low = jnp.where(ok, 0.0, LOW).astype(F32)
                pieces.append(s[:, j * tile : (j + 1) * tile] * scale + low)
        top = pieces[0]
        for x in pieces[1:]:
            top = jnp.maximum(top, x)
        top = jnp.max(top, axis=1, keepdims=True)
        pieces = [jnp.exp(x - top) for x in pieces]
        total = pieces[0]
        for x in pieces[1:]:
            total = total + x
        total = jnp.sum(total, axis=1, keepdims=True)
        o_sum = None
        for o in range(3):
            p = jnp.concatenate([x.astype(BF) for x in pieces[o * tiles : (o + 1) * tiles]], axis=1)
            part = jnp.dot(p, frames[o][:, 128:256], preferred_element_type=F32)
            o_sum = part if o_sum is None else o_sum + part
        out_ref[rows, :] = (o_sum / total * own_live).astype(BF)


def spatial(kind, mask, valid, place, q, own, before, after, first, count, channels, scale, tile):
    tokens = q.shape[0]
    heads = kind.shape[0]
    size = channels // heads

    def slot(i, *_):
        return (0, i)

    return pl.pallas_call(
        functools.partial(spatial_kernel, scale, tile, first),
        grid_spec=pltpu.PrefetchScalarGridSpec(
            num_scalar_prefetch=4,
            grid=(count,),
            in_specs=[pl.BlockSpec((tokens, size), slot)]
            + [pl.BlockSpec((tokens, 2 * size), slot)] * 3,
            out_specs=pl.BlockSpec(
                (tokens, size),
                lambda i, kind_ref, *_: (0, head_at(first + i, kind_ref, heads)),
            ),
        ),
        out_shape=jax.ShapeDtypeStruct((tokens, channels), BF),
        compiler_params=params(),
        cost_estimate=pl.CostEstimate(
            flops=12 * tokens * tokens * size * count,
            bytes_accessed=16 * tokens * size * count,
            transcendentals=3 * tokens * tokens * count,
        ),
        name="spatial_heads",
    )(kind, mask, valid, place, q, own, before, after)


def merge_kernel(count, kind_ref, base_ref, x_ref, out_ref, sems):
    heads = kind_ref.shape[0]
    size = out_ref.shape[1] // heads
    copies = []
    for s in range(count):
        start = pl.multiple_of(head_at(s, kind_ref, heads) * size, size)
        copy = pltpu.make_async_copy(
            x_ref.at[:, pl.ds(s * size, size)], out_ref.at[:, pl.ds(start, size)], sems.at[s]
        )
        copy.start()
        copies.append(copy)
    for copy in copies:
        copy.wait()


def merge(kind, base, x, count):
    return pl.pallas_call(
        functools.partial(merge_kernel, count),
        in_specs=[pl.BlockSpec(memory_space=pltpu.SMEM)]
        + [pl.BlockSpec(memory_space=pl.ANY)] * 2,
        out_specs=pl.BlockSpec(memory_space=pl.ANY),
        out_shape=jax.ShapeDtypeStruct(base.shape, BF),
        scratch_shapes=[pltpu.SemaphoreType.DMA((count,))],
        input_output_aliases={1: 0},
        compiler_params=params(),
        cost_estimate=pl.CostEstimate(flops=0, bytes_accessed=4 * x.size, transcendentals=0),
        name="merge_heads",
    )(kind, base, x)


def local(queries, keys, values, gain_q, gain_k, head_kind, tile_mask, frame_valid):
    heads = head_kind.shape[0]
    tokens, channels = queries.shape[1:]
    size = channels // heads
    tile = tokens // tile_mask.shape[1]
    frames = lax.axis_size("frames")
    blocks = lax.axis_size("heads")
    position = lax.axis_index("frames")
    scale = 1.0 / math.sqrt(size)
    share = tokens // frames
    q, k, v = queries[0], keys[0], values[0]

    parts = local_sums(q, k, blocks, tile)
    parts = lax.all_to_all(parts, "heads", split_axis=0, concat_axis=0, tiled=True)

    place = position[None]
    valid_row = frame_valid[None, :]
    up = [(i, i + 1) for i in range(frames - 1)]
    down = [(j, i) for i, j in up]

    def exchange(x):
        x = x.reshape(frames, share, x.shape[1])
        return lax.all_to_all(x, "frames", split_axis=0, concat_axis=0, tiled=True).reshape(
            tokens, x.shape[2]
        )

    def branch(count):
        rest = heads - count

        def run(q, k, v, parts):
            args = (head_kind, parts, gain_q, gain_k, q, k, v)
            (sent,) = pack(*args, 0, count, True, blocks * channels, tile)
            mine = exchange(sent)
            pair, near_q = pack(*args, count, rest, False, blocks * channels, tile)
            earlier = lax.ppermute(pair, "frames", up)
            later = lax.ppermute(pair, "frames", down)
            told = temporal(mine, valid_row, (earlier, later), count, share, size, scale)
            back = exchange(told)
            base = spatial(
                head_kind, tile_mask, frame_valid, place, near_q, pair, earlier, later,
                count, rest, channels, scale, tile,
            )
            return merge(head_kind, base, back, count)

        return run

    choice = jnp.sum(head_kind) - 1
    out = lax.switch(choice, [branch(c) for c in range(1, heads)], q, k, v, parts)
    return out[None]


def solution(mesh):
    placed = (
        P("frames", None, "heads"),
        P("frames", None, "heads"),
        P("frames", None, "heads"),
        P("heads"),
        P("heads"),
        P("heads"),
        P("heads", None, None),
        P(),
    )
    return jax.shard_map(
        local, mesh=mesh, in_specs=placed, out_specs=P("frames", None, "heads"), check_vma=False
    )
```

```python
import functools
import math

import jax
import jax.numpy as jnp
from jax import lax
from jax.experimental import pallas as pl
from jax.experimental.pallas import tpu as pltpu
from jax.sharding import PartitionSpec as P

epsilon = 1e-06
VIDEO = 32
SHIFT = 8
LOW = -1e30
BF = jnp.bfloat16
F32 = jnp.float32


def params():
    return pltpu.CompilerParams(vmem_limit_bytes=40 * 1024 * 1024)


def head_at(slot, kind_ref, heads):
    flags = [kind_ref[h] for h in range(heads)]
    total = sum(flags)
    found = jnp.int32(0)
    seen = jnp.int32(0)
    for h in range(heads):
        rank = jnp.where(flags[h] > 0, seen, total + h - seen)
        found = jnp.where(rank == slot, h, found)
        seen = seen + flags[h]
    return found


def sums_kernel(groups, tile, q_ref, k_ref, out_ref, q_buf, k_buf, sems):
    tokens = q_ref.shape[0]
    steps = tokens // tile
    copies = []
    for i in range(steps):
        rows = pl.ds(i * tile, tile)
        for n, (ref, buf) in enumerate(((q_ref, q_buf), (k_ref, k_buf))):
            copy = pltpu.make_async_copy(ref.at[rows, :], buf.at[rows, :], sems.at[2 * i + n])
            copy.start()
            copies.append(copy)
    for i in range(steps):
        for n, buf in enumerate((q_buf, k_buf)):
            copies[2 * i + n].wait()
            x = buf[pl.ds(i * tile, tile), :].astype(F32)
            x = x * x
            part = x[:, :128]
            for g in range(1, groups):
                part = part + x[:, g * 128 : (g + 1) * 128]
            row = jnp.sum(part.T, axis=0, keepdims=True)
            at = n * steps + i
            out_ref[:, at : at + 1, :] = jnp.broadcast_to(row[None], (out_ref.shape[0], 1, tile))


def local_sums(q, k, copies, tile):
    tokens, channels = q.shape
    steps = tokens // tile
    return pl.pallas_call(
        functools.partial(sums_kernel, channels // 128, tile),
        in_specs=[pl.BlockSpec(memory_space=pl.ANY)] * 2,
        out_specs=pl.BlockSpec(memory_space=pltpu.VMEM),
        out_shape=jax.ShapeDtypeStruct((copies, 2 * steps, tile), F32),
        scratch_shapes=[pltpu.VMEM((tokens, channels), BF)] * 2
        + [pltpu.SemaphoreType.DMA((2 * steps,))],
        compiler_params=params(),
        cost_estimate=pl.CostEstimate(
            flops=4 * q.size, bytes_accessed=4 * q.size, transcendentals=0
        ),
        name="square_sums",
    )(q, k)


def pack_kernel(
    all_channels, tile, first, count, joined,
    kind_ref, parts_ref, gq_ref, gk_ref, q_ref, k_ref, v_ref, *rest
):
    if joined:
        out_ref, q_buf, k_buf, out_buf, rq, rk, in_sems, out_sems = rest[-8:]
    else:
        out_ref, qn_ref, q_buf, k_buf, out_buf, rq, rk, in_sems, out_sems = rest[-9:]
    tokens = q_ref.shape[0]
    heads = kind_ref.shape[0]
    size = q_ref.shape[1] // heads
    width = out_buf.shape[2]

    def column(s):
        return pl.multiple_of(head_at(first + s, kind_ref, heads) * size, size)

    def loads(s):
        columns = pl.ds(column(s), size)
        trio = (
            (q_ref, q_buf.at[s]),
            (k_ref, k_buf.at[s]),
            (v_ref, out_buf.at[s, :, pl.ds(width - size, size)]),
        )
        return [
            pltpu.make_async_copy(ref.at[:, columns], buf, in_sems.at[3 * s + n])
            for n, (ref, buf) in enumerate(trio)
        ]

    def stores(s):
        columns = pl.ds(pl.multiple_of(s * width, width), width)
        return pltpu.make_async_copy(out_buf.at[s], out_ref.at[:, columns], out_sems.at[s])

    def begin(s, carry):
        for copy in loads(s):
            copy.start()
        return carry

    lax.fori_loop(0, count, begin, 0)
    total = jnp.sum(parts_ref[...], axis=0)
    scale = lax.rsqrt(total / all_channels + epsilon)
    rows = tokens // tile
    for c in range(rows):
        here = pl.ds(c * tile, tile)
        rq[here, :] = jnp.broadcast_to(scale[c : c + 1, :], (tile, tile)).T
        rk[here, :] = jnp.broadcast_to(scale[rows + c : rows + c + 1, :], (tile, tile)).T

    def work(s, carry):
        gain_q = gq_ref[pl.ds(column(s), size)].reshape(1, size)
        gain_k = gk_ref[pl.ds(column(s), size)].reshape(1, size)
        copies = loads(s)
        copies[0].wait()
        normed_q = (q_buf[s].astype(F32) * rq[...] * gain_q).astype(BF)
        copies[1].wait()
        normed_k = (k_buf[s].astype(F32) * rk[...] * gain_k).astype(BF)
        if joined:
            out_buf[s, :, 0:size] = normed_q
            out_buf[s, :, size : 2 * size] = normed_k
        else:
            columns = pl.ds(pl.multiple_of(s * size, size), size)
            qn_ref[:, columns] = normed_q
            out_buf[s, :, 0:size] = normed_k
        copies[2].wait()
        stores(s).start()
        return carry

    lax.fori_loop(0, count, work, 0)

    def end(s, carry):
        stores(s).wait()
        return carry

    lax.fori_loop(0, count, end, 0)


def pack(kind, parts, gain_q, gain_k, q, k, v, after, first, count, joined, all_channels, tile):
    tokens, channels = q.shape
    size = channels // kind.shape[0]
    width = (3 if joined else 2) * size
    out_shape = [jax.ShapeDtypeStruct((tokens, count * width), BF)]
    out_specs = [pl.BlockSpec(memory_space=pl.ANY)]
    if not joined:
        out_shape.append(jax.ShapeDtypeStruct((tokens, count * size), BF))
        out_specs.append(pl.BlockSpec(memory_space=pltpu.VMEM))
    return pl.pallas_call(
        functools.partial(pack_kernel, all_channels, tile, first, count, joined),
        in_specs=[pl.BlockSpec(memory_space=pltpu.SMEM)]
        + [pl.BlockSpec(memory_space=pltpu.VMEM)] * 3
        + [pl.BlockSpec(memory_space=pl.ANY)] * (3 + len(after)),
        out_specs=out_specs,
        out_shape=out_shape,
        scratch_shapes=[
            pltpu.VMEM((count, tokens, size), BF),
            pltpu.VMEM((count, tokens, size), BF),
            pltpu.VMEM((count, tokens, width), BF),
            pltpu.VMEM((tokens, size), F32),
            pltpu.VMEM((tokens, size), F32),
            pltpu.SemaphoreType.DMA((3 * count,)),
            pltpu.SemaphoreType.DMA((count,)),
        ],
        compiler_params=params(),
        cost_estimate=pl.CostEstimate(
            flops=4 * tokens * size * count,
            bytes_accessed=12 * tokens * size * count,
            transcendentals=0,
        ),
        name="pack_temporal" if joined else "pack_spatial",
    )(kind, parts, gain_q, gain_k, q, k, v, *after)


def video_rows(frames, share):
    spans = []
    start = 0
    while start < frames:
        stop = min(frames, ((start + SHIFT) // VIDEO + 1) * VIDEO - SHIFT)
        spans.append((start * share, stop * share))
        start = stop
    return spans


def temporal_kernel(scale, count, share, x_ref, valid_ref, *rest):
    spans = video_rows(valid_ref.shape[1], share)
    out_ref, x_buf, out_buf, live_buf, *masks = rest[-6 - len(spans) : -2]
    in_sems, out_sems = rest[-2:]
    rows = x_ref.shape[0]
    frames = valid_ref.shape[1]
    size = out_buf.shape[2]

    def load(s):
        columns = pl.ds(pl.multiple_of(s * 3 * size, 3 * size), 3 * size)
        return pltpu.make_async_copy(x_ref.at[:, columns], x_buf.at[s], in_sems.at[s])

    def begin(s, carry):
        load(s).start()
        return carry

    lax.fori_loop(0, count, begin, 0)
    bits = share.bit_length() - 1
    live = jnp.where(valid_ref[...] > 0, 1.0, 0.0).astype(F32)
    owner = lax.broadcasted_iota(jnp.int32, (rows, frames), 0) >> bits
    hot = jnp.where(owner == lax.broadcasted_iota(jnp.int32, (rows, frames), 1), 1.0, 0.0)
    hot = hot.astype(BF)
    over = (((1,), (1,)), ((), ()))
    live_row = lax.dot_general(
        jnp.broadcast_to(live, (8, frames)).astype(BF), hot, over, preferred_element_type=F32
    )
    live_buf[...] = lax.dot_general(
        hot, jnp.broadcast_to(live, (size, frames)).astype(BF), over, preferred_element_type=F32
    )
    for (low, high), mask in zip(spans, masks):
        n = high - low
        at_row = lax.broadcasted_iota(jnp.int32, (n, n), 0)
        at_col = lax.broadcasted_iota(jnp.int32, (n, n), 1)
        same_token = ((at_row ^ at_col) & (share - 1)) == 0
        allowed = same_token & ((live_row[0:1, low:high] > 0.5) | (at_row == at_col))
        mask[...] = jnp.where(allowed, 0.0, LOW).astype(F32)

    def store(s):
        columns = pl.ds(pl.multiple_of(s * size, size), size)
        return pltpu.make_async_copy(out_buf.at[s], out_ref.at[:, columns], out_sems.at[s])

    for s in range(count):
        load(s).wait()
    for s in range(count):
        for (low, high), mask in zip(spans, masks):
            here = pl.ds(low, high - low)
            x = lax.dot_general(
                x_buf[s, here, 0:size],
                x_buf[s, here, size : 2 * size],
                over,
                preferred_element_type=F32,
            )
            x = x + mask[...]
            p = jnp.exp2((x - jnp.max(x, axis=1, keepdims=True)) * scale)
            total = jnp.sum(p, axis=1, keepdims=True)
            o = jnp.dot(
                p.astype(BF), x_buf[s, here, 2 * size : 3 * size], preferred_element_type=F32
            )
            out_buf[s, here, :] = (o / total * live_buf[here, :]).astype(BF)
        store(s).start()

    def end(s, carry):
        store(s).wait()
        return carry

    lax.fori_loop(0, count, end, 0)


def temporal(x, valid_row, after, count, share, size, scale):
    rows = x.shape[0]
    return pl.pallas_call(
        functools.partial(temporal_kernel, scale, count, share),
        in_specs=[
            pl.BlockSpec(memory_space=pl.ANY),
            pl.BlockSpec(memory_space=pltpu.VMEM),
        ]
        + [pl.BlockSpec(memory_space=pl.ANY)] * len(after),
        out_specs=pl.BlockSpec(memory_space=pl.ANY),
        out_shape=jax.ShapeDtypeStruct((rows, count * size), BF),
        scratch_shapes=[
            pltpu.VMEM((count, rows, 3 * size), BF),
            pltpu.VMEM((count, rows, size), BF),
            pltpu.VMEM((rows, size), F32),
            *[
                pltpu.VMEM((high - low, high - low), F32)
                for low, high in video_rows(valid_row.shape[1], share)
            ],
            pltpu.SemaphoreType.DMA((count,)),
            pltpu.SemaphoreType.DMA((count,)),
        ],
        compiler_params=params(),
        cost_estimate=pl.CostEstimate(
            flops=4 * rows * rows * size * count,
            bytes_accessed=8 * rows * size * count,
            transcendentals=rows * rows * count,
        ),
        name="temporal_heads",
    )(x, valid_row, *after)


def spatial_kernel(
    scale, tile, first, kind_ref, mask_ref, valid_ref, place_ref,
    q_ref, own_ref, before_ref, after_ref, out_ref
):
    heads = kind_ref.shape[0]
    head = head_at(first + pl.program_id(0), kind_ref, heads)
    tiles = own_ref.shape[0] // tile
    i = pl.program_id(1)
    frames = (before_ref, own_ref, after_ref)
    place = place_ref[0]
    last = valid_ref.shape[0] - 1
    near = [None, jnp.bool_(True), None]
    for o, there in ((0, jnp.maximum(place - 1, 0)), (2, jnp.minimum(place + 1, last))):
        same = ((there + SHIFT) // VIDEO == (place + SHIFT) // VIDEO) & (there != place)
        near[o] = same & (valid_ref[there] > 0)
    own_live = jnp.where(valid_ref[place] > 0, 1.0, 0.0).astype(F32)
    q = q_ref[...]
    pieces = []
    for o in range(3):
        s = lax.dot_general(
            q, frames[o][:, 0:128], (((1,), (1,)), ((), ())), preferred_element_type=F32
        )
        for j in range(tiles):
            ok = (mask_ref[head, i, o * tiles + j] > 0) & near[o]
            low = jnp.where(ok, 0.0, LOW).astype(F32)
            pieces.append(s[:, j * tile : (j + 1) * tile] + low)
    top = pieces[0]
    for x in pieces[1:]:
        top = jnp.maximum(top, x)
    top = jnp.max(top, axis=1, keepdims=True)
    pieces = [jnp.exp2((x - top) * scale) for x in pieces]
    total = pieces[0]
    for x in pieces[1:]:
        total = total + x
    total = jnp.sum(total, axis=1, keepdims=True)
    o_sum = None
    for o in range(3):
        p = jnp.concatenate([x.astype(BF) for x in pieces[o * tiles : (o + 1) * tiles]], axis=1)
        part = jnp.dot(p, frames[o][:, 128:256], preferred_element_type=F32)
        o_sum = part if o_sum is None else o_sum + part
    out_ref[...] = (o_sum / total * own_live).astype(BF)


def spatial(kind, mask, valid, place, q, own, before, after, first, count, channels, scale, tile):
    tokens = q.shape[0]
    heads = kind.shape[0]
    size = channels // heads

    def slot(i, j, *_):
        return (0, i)

    return pl.pallas_call(
        functools.partial(spatial_kernel, scale, tile, first),
        grid_spec=pltpu.PrefetchScalarGridSpec(
            num_scalar_prefetch=4,
            grid=(count, tokens // tile),
            in_specs=[pl.BlockSpec((tile, size), lambda i, j, *_: (j, i))]
            + [pl.BlockSpec((tokens, 2 * size), slot)] * 3,
            out_specs=pl.BlockSpec(
                (tile, size),
                lambda i, j, kind_ref, *_: (j, head_at(first + i, kind_ref, heads)),
            ),
        ),
        out_shape=jax.ShapeDtypeStruct((tokens, channels), BF),
        compiler_params=params(),
        cost_estimate=pl.CostEstimate(
            flops=12 * tokens * tokens * size * count,
            bytes_accessed=16 * tokens * size * count,
            transcendentals=3 * tokens * tokens * count,
        ),
        name="spatial_heads",
    )(kind, mask, valid, place, q, own, before, after)


def merge_kernel(count, kind_ref, base_ref, x_ref, out_ref, sems):
    heads = kind_ref.shape[0]
    size = out_ref.shape[1] // heads
    copies = []
    for s in range(count):
        start = pl.multiple_of(head_at(s, kind_ref, heads) * size, size)
        copy = pltpu.make_async_copy(
            x_ref.at[:, pl.ds(s * size, size)], out_ref.at[:, pl.ds(start, size)], sems.at[s]
        )
        copy.start()
        copies.append(copy)
    for copy in copies:
        copy.wait()


def merge(kind, base, x, count):
    return pl.pallas_call(
        functools.partial(merge_kernel, count),
        in_specs=[pl.BlockSpec(memory_space=pltpu.SMEM)]
        + [pl.BlockSpec(memory_space=pltpu.HBM), pl.BlockSpec(memory_space=pl.ANY)],
        out_specs=pl.BlockSpec(memory_space=pltpu.HBM),
        out_shape=jax.ShapeDtypeStruct(base.shape, BF),
        scratch_shapes=[pltpu.SemaphoreType.DMA((count,))],
        input_output_aliases={1: 0},
        compiler_params=params(),
        cost_estimate=pl.CostEstimate(flops=0, bytes_accessed=4 * x.size, transcendentals=0),
        name="merge_heads",
    )(kind, base, x)


def local(queries, keys, values, gain_q, gain_k, head_kind, tile_mask, frame_valid):
    heads = head_kind.shape[0]
    tokens, channels = queries.shape[1:]
    size = channels // heads
    tile = tokens // tile_mask.shape[1]
    frames = lax.axis_size("frames")
    blocks = lax.axis_size("heads")
    position = lax.axis_index("frames")
    scale = math.log2(math.e) / math.sqrt(size)
    share = tokens // frames
    q, k, v = queries[0], keys[0], values[0]

    parts = local_sums(q, k, blocks, tile)
    parts = lax.all_to_all(parts, "heads", split_axis=0, concat_axis=0, tiled=True)

    place = position[None]
    valid_row = frame_valid[None, :]
    up = [(i, i + 1) for i in range(frames - 1)]
    down = [(j, i) for i, j in up]

    def exchange(x):
        x = x.reshape(frames, share, x.shape[1])
        return lax.all_to_all(x, "frames", split_axis=0, concat_axis=0, tiled=True).reshape(
            tokens, x.shape[2]
        )

    def branch(count, late):
        rest = heads - count

        def run(q, k, v, parts):
            args = (head_kind, parts, gain_q, gain_k, q, k, v)

            def near():
                pair, near_q = pack(*args, (), count, rest, False, blocks * channels, tile)
                earlier = lax.ppermute(pair, "frames", up)
                later = lax.ppermute(pair, "frames", down)
                return near_q, pair, earlier, later

            def attend(near_q, pair, earlier, later):
                return spatial(
                    head_kind, tile_mask, frame_valid, place, near_q, pair, earlier, later,
                    count, rest, channels, scale, tile,
                )

            def send(*after):
                (sent,) = pack(*args, after, 0, count, True, blocks * channels, tile)
                return exchange(sent)

            if late == 0:
                mine = send()
                found = near()
                after = found[2:]
            elif late == 1:
                found = near()
                mine = send(*found[2:])
                after = ()
            else:
                found = near()
                base = attend(*found)
                mine = send(base)
                after = ()
            told = temporal(mine, valid_row, after, count, share, size, scale)
            back = exchange(told)
            if late < 2:
                base = attend(*found)
            return merge(head_kind, base, back, count)

        return run

    count = jnp.sum(head_kind)
    odd = lax.axis_index("heads") % 2
    choice = count - 1 + jnp.where((odd == 1) & (count > 2), heads - 3, 0)
    branches = [branch(c, 0) for c in range(1, heads)]
    branches += [branch(c, 2) for c in range(3, heads)]
    out = lax.switch(choice, branches, q, k, v, parts)
    return out[None]


def solution(mesh):
    placed = (
        P("frames", None, "heads"),
        P("frames", None, "heads"),
        P("frames", None, "heads"),
        P("heads"),
        P("heads"),
        P("heads"),
        P("heads", None, None),
        P(),
    )
    return jax.shard_map(
        local, mesh=mesh, in_specs=placed, out_specs=P("frames", None, "heads"), check_vma=False
    )
```

```python
import functools
import math

import jax
import jax.numpy as jnp
from jax import lax
from jax.experimental import pallas as pl
from jax.experimental.pallas import tpu as pltpu
from jax.sharding import PartitionSpec as P

epsilon = 1e-06
VIDEO = 32
SHIFT = 8
LOW = -1e30
BF = jnp.bfloat16
F32 = jnp.float32


def params():
    return pltpu.CompilerParams(vmem_limit_bytes=40 * 1024 * 1024)


def head_at(slot, kind_ref, heads):
    flags = [kind_ref[h] for h in range(heads)]
    total = sum(flags)
    found = jnp.int32(0)
    seen = jnp.int32(0)
    for h in range(heads):
        rank = jnp.where(flags[h] > 0, seen, total + h - seen)
        found = jnp.where(rank == slot, h, found)
        seen = seen + flags[h]
    return found


def sums_kernel(groups, tile, q_ref, k_ref, out_ref, q_buf, k_buf, sems):
    tokens = q_ref.shape[0]
    steps = tokens // tile
    copies = []
    for i in range(steps):
        rows = pl.ds(i * tile, tile)
        for n, (ref, buf) in enumerate(((q_ref, q_buf), (k_ref, k_buf))):
            copy = pltpu.make_async_copy(ref.at[rows, :], buf.at[rows, :], sems.at[2 * i + n])
            copy.start()
            copies.append(copy)
    for i in range(steps):
        for n, buf in enumerate((q_buf, k_buf)):
            copies[2 * i + n].wait()
            x = buf[pl.ds(i * tile, tile), :].astype(F32)
            x = x * x
            part = x[:, :128]
            for g in range(1, groups):
                part = part + x[:, g * 128 : (g + 1) * 128]
            row = jnp.sum(part.T, axis=0, keepdims=True)
            at = n * steps + i
            out_ref[:, at : at + 1, :] = jnp.broadcast_to(row[None], (out_ref.shape[0], 1, tile))


def local_sums(q, k, copies, tile):
    tokens, channels = q.shape
    steps = tokens // tile
    return pl.pallas_call(
        functools.partial(sums_kernel, channels // 128, tile),
        in_specs=[pl.BlockSpec(memory_space=pl.ANY)] * 2,
        out_specs=pl.BlockSpec(memory_space=pltpu.VMEM),
        out_shape=jax.ShapeDtypeStruct((copies, 2 * steps, tile), F32),
        scratch_shapes=[pltpu.VMEM((tokens, channels), BF)] * 2
        + [pltpu.SemaphoreType.DMA((2 * steps,))],
        compiler_params=params(),
        cost_estimate=pl.CostEstimate(
            flops=4 * q.size, bytes_accessed=4 * q.size, transcendentals=0
        ),
        name="square_sums",
    )(q, k)


def pack_kernel(
    all_channels, tile, first, count, joined,
    kind_ref, parts_ref, gq_ref, gk_ref, q_ref, k_ref, v_ref, *rest
):
    if joined:
        out_ref, q_buf, k_buf, out_buf, rq, rk, in_sems, out_sems = rest[-8:]
    else:
        out_ref, qn_ref, q_buf, k_buf, out_buf, rq, rk, in_sems, out_sems = rest[-9:]
    tokens = q_ref.shape[0]
    heads = kind_ref.shape[0]
    size = q_ref.shape[1] // heads
    width = out_buf.shape[2]

    def column(s):
        return pl.multiple_of(head_at(first + s, kind_ref, heads) * size, size)

    def loads(s):
        columns = pl.ds(column(s), size)
        trio = (
            (q_ref, q_buf.at[s]),
            (k_ref, k_buf.at[s]),
            (v_ref, out_buf.at[s, :, pl.ds(width - size, size)]),
        )
        return [
            pltpu.make_async_copy(ref.at[:, columns], buf, in_sems.at[3 * s + n])
            for n, (ref, buf) in enumerate(trio)
        ]

    def stores(s):
        columns = pl.ds(pl.multiple_of(s * width, width), width)
        return pltpu.make_async_copy(out_buf.at[s], out_ref.at[:, columns], out_sems.at[s])

    def begin(s, carry):
        for copy in loads(s):
            copy.start()
        return carry

    lax.fori_loop(0, count, begin, 0)
    total = jnp.sum(parts_ref[...], axis=0)
    scale = lax.rsqrt(total / all_channels + epsilon)
    rows = tokens // tile
    for c in range(rows):
        here = pl.ds(c * tile, tile)
        rq[here, :] = jnp.broadcast_to(scale[c : c + 1, :], (tile, tile)).T
        rk[here, :] = jnp.broadcast_to(scale[rows + c : rows + c + 1, :], (tile, tile)).T

    def work(s, carry):
        gain_q = gq_ref[pl.ds(column(s), size)].reshape(1, size)
        gain_k = gk_ref[pl.ds(column(s), size)].reshape(1, size)
        copies = loads(s)
        copies[0].wait()
        normed_q = (q_buf[s].astype(F32) * rq[...] * gain_q).astype(BF)
        copies[1].wait()
        normed_k = (k_buf[s].astype(F32) * rk[...] * gain_k).astype(BF)
        if joined:
            out_buf[s, :, 0:size] = normed_q
            out_buf[s, :, size : 2 * size] = normed_k
        else:
            columns = pl.ds(pl.multiple_of(s * size, size), size)
            qn_ref[:, columns] = normed_q
            out_buf[s, :, 0:size] = normed_k
        copies[2].wait()
        stores(s).start()
        return carry

    lax.fori_loop(0, count, work, 0)

    def end(s, carry):
        stores(s).wait()
        return carry

    lax.fori_loop(0, count, end, 0)


def pack(kind, parts, gain_q, gain_k, q, k, v, after, first, count, joined, all_channels, tile):
    tokens, channels = q.shape
    size = channels // kind.shape[0]
    width = (3 if joined else 2) * size
    out_shape = [jax.ShapeDtypeStruct((tokens, count * width), BF)]
    out_specs = [pl.BlockSpec(memory_space=pl.ANY)]
    if not joined:
        out_shape.append(jax.ShapeDtypeStruct((tokens, count * size), BF))
        out_specs.append(pl.BlockSpec(memory_space=pltpu.VMEM))
    return pl.pallas_call(
        functools.partial(pack_kernel, all_channels, tile, first, count, joined),
        in_specs=[pl.BlockSpec(memory_space=pltpu.SMEM)]
        + [pl.BlockSpec(memory_space=pltpu.VMEM)] * 3
        + [pl.BlockSpec(memory_space=pl.ANY)] * (3 + len(after)),
        out_specs=out_specs,
        out_shape=out_shape,
        scratch_shapes=[
            pltpu.VMEM((count, tokens, size), BF),
            pltpu.VMEM((count, tokens, size), BF),
            pltpu.VMEM((count, tokens, width), BF),
            pltpu.VMEM((tokens, size), F32),
            pltpu.VMEM((tokens, size), F32),
            pltpu.SemaphoreType.DMA((3 * count,)),
            pltpu.SemaphoreType.DMA((count,)),
        ],
        compiler_params=params(),
        cost_estimate=pl.CostEstimate(
            flops=4 * tokens * size * count,
            bytes_accessed=12 * tokens * size * count,
            transcendentals=0,
        ),
        name="pack_temporal" if joined else "pack_spatial",
    )(kind, parts, gain_q, gain_k, q, k, v, *after)


def video_rows(frames, share):
    spans = []
    start = 0
    while start < frames:
        stop = min(frames, ((start + SHIFT) // VIDEO + 1) * VIDEO - SHIFT)
        spans.append((start * share, stop * share))
        start = stop
    return spans


def temporal_kernel(scale, count, share, x_ref, valid_ref, *rest):
    spans = video_rows(valid_ref.shape[1], share)
    out_ref, x_buf, out_buf, live_buf, *masks = rest[-6 - len(spans) : -2]
    in_sems, out_sems = rest[-2:]
    rows = x_ref.shape[0]
    frames = valid_ref.shape[1]
    size = out_buf.shape[2]

    def load(s):
        columns = pl.ds(pl.multiple_of(s * 3 * size, 3 * size), 3 * size)
        return pltpu.make_async_copy(x_ref.at[:, columns], x_buf.at[s], in_sems.at[s])

    def begin(s, carry):
        load(s).start()
        return carry

    lax.fori_loop(0, count, begin, 0)
    bits = share.bit_length() - 1
    live = jnp.where(valid_ref[...] > 0, 1.0, 0.0).astype(F32)
    owner = lax.broadcasted_iota(jnp.int32, (rows, frames), 0) >> bits
    hot = jnp.where(owner == lax.broadcasted_iota(jnp.int32, (rows, frames), 1), 1.0, 0.0)
    hot = hot.astype(BF)
    over = (((1,), (1,)), ((), ()))
    live_row = lax.dot_general(
        jnp.broadcast_to(live, (8, frames)).astype(BF), hot, over, preferred_element_type=F32
    )
    live_buf[...] = lax.dot_general(
        hot, jnp.broadcast_to(live, (size, frames)).astype(BF), over, preferred_element_type=F32
    )
    for (low, high), mask in zip(spans, masks):
        n = high - low
        at_row = lax.broadcasted_iota(jnp.int32, (n, n), 0)
        at_col = lax.broadcasted_iota(jnp.int32, (n, n), 1)
        same_token = ((at_row ^ at_col) & (share - 1)) == 0
        allowed = same_token & ((live_row[0:1, low:high] > 0.5) | (at_row == at_col))
        mask[...] = jnp.where(allowed, 0.0, LOW).astype(F32)

    def store(s):
        columns = pl.ds(pl.multiple_of(s * size, size), size)
        return pltpu.make_async_copy(out_buf.at[s], out_ref.at[:, columns], out_sems.at[s])

    for s in range(count):
        load(s).wait()
    for s in range(count):
        for (low, high), mask in zip(spans, masks):
            here = pl.ds(low, high - low)
            x = lax.dot_general(
                x_buf[s, here, 0:size],
                x_buf[s, here, size : 2 * size],
                over,
                preferred_element_type=F32,
            )
            x = x + mask[...]
            p = jnp.exp2((x - jnp.max(x, axis=1, keepdims=True)) * scale)
            total = jnp.sum(p, axis=1, keepdims=True)
            o = jnp.dot(
                p.astype(BF), x_buf[s, here, 2 * size : 3 * size], preferred_element_type=F32
            )
            out_buf[s, here, :] = (o / total * live_buf[here, :]).astype(BF)
        store(s).start()

    def end(s, carry):
        store(s).wait()
        return carry

    lax.fori_loop(0, count, end, 0)


def temporal(x, valid_row, after, count, share, size, scale):
    rows = x.shape[0]
    return pl.pallas_call(
        functools.partial(temporal_kernel, scale, count, share),
        in_specs=[
            pl.BlockSpec(memory_space=pl.ANY),
            pl.BlockSpec(memory_space=pltpu.VMEM),
        ]
        + [pl.BlockSpec(memory_space=pl.ANY)] * len(after),
        out_specs=pl.BlockSpec(memory_space=pl.ANY),
        out_shape=jax.ShapeDtypeStruct((rows, count * size), BF),
        scratch_shapes=[
            pltpu.VMEM((count, rows, 3 * size), BF),
            pltpu.VMEM((count, rows, size), BF),
            pltpu.VMEM((rows, size), F32),
            *[
                pltpu.VMEM((high - low, high - low), F32)
                for low, high in video_rows(valid_row.shape[1], share)
            ],
            pltpu.SemaphoreType.DMA((count,)),
            pltpu.SemaphoreType.DMA((count,)),
        ],
        compiler_params=params(),
        cost_estimate=pl.CostEstimate(
            flops=4 * rows * rows * size * count,
            bytes_accessed=8 * rows * size * count,
            transcendentals=rows * rows * count,
        ),
        name="temporal_heads",
    )(x, valid_row, *after)


def spatial_kernel(
    scale, tile, first, kind_ref, mask_ref, valid_ref, place_ref,
    q_ref, own_ref, before_ref, after_ref, out_ref
):
    heads = kind_ref.shape[0]
    head = head_at(first + pl.program_id(0), kind_ref, heads)
    tiles = own_ref.shape[0] // tile
    i = pl.program_id(1)
    frames = (before_ref, own_ref, after_ref)
    place = place_ref[0]
    last = valid_ref.shape[0] - 1
    near = [None, jnp.bool_(True), None]
    for o, there in ((0, jnp.maximum(place - 1, 0)), (2, jnp.minimum(place + 1, last))):
        same = ((there + SHIFT) // VIDEO == (place + SHIFT) // VIDEO) & (there != place)
        near[o] = same & (valid_ref[there] > 0)
    own_live = jnp.where(valid_ref[place] > 0, 1.0, 0.0).astype(F32)
    q = q_ref[...]
    pieces = []
    for o in range(3):
        s = lax.dot_general(
            q, frames[o][:, 0:128], (((1,), (1,)), ((), ())), preferred_element_type=F32
        )
        for j in range(tiles):
            ok = (mask_ref[head, i, o * tiles + j] > 0) & near[o]
            low = jnp.where(ok, 0.0, LOW).astype(F32)
            pieces.append(s[:, j * tile : (j + 1) * tile] + low)
    top = pieces[0]
    for x in pieces[1:]:
        top = jnp.maximum(top, x)
    top = jnp.max(top, axis=1, keepdims=True)
    pieces = [jnp.exp2((x - top) * scale) for x in pieces]
    total = pieces[0]
    for x in pieces[1:]:
        total = total + x
    total = jnp.sum(total, axis=1, keepdims=True)
    o_sum = None
    for o in range(3):
        p = jnp.concatenate([x.astype(BF) for x in pieces[o * tiles : (o + 1) * tiles]], axis=1)
        part = jnp.dot(p, frames[o][:, 128:256], preferred_element_type=F32)
        o_sum = part if o_sum is None else o_sum + part
    out_ref[...] = (o_sum / total * own_live).astype(BF)


def spatial(kind, mask, valid, place, q, own, before, after, first, count, channels, scale, tile):
    tokens = q.shape[0]
    heads = kind.shape[0]
    size = channels // heads

    def slot(i, j, *_):
        return (0, i)

    return pl.pallas_call(
        functools.partial(spatial_kernel, scale, tile, first),
        grid_spec=pltpu.PrefetchScalarGridSpec(
            num_scalar_prefetch=4,
            grid=(count, tokens // tile),
            in_specs=[pl.BlockSpec((tile, size), lambda i, j, *_: (j, i))]
            + [pl.BlockSpec((tokens, 2 * size), slot)] * 3,
            out_specs=pl.BlockSpec(
                (tile, size),
                lambda i, j, kind_ref, *_: (j, head_at(first + i, kind_ref, heads)),
            ),
        ),
        out_shape=jax.ShapeDtypeStruct((tokens, channels), BF),
        compiler_params=params(),
        cost_estimate=pl.CostEstimate(
            flops=12 * tokens * tokens * size * count,
            bytes_accessed=16 * tokens * size * count,
            transcendentals=3 * tokens * tokens * count,
        ),
        name="spatial_heads",
    )(kind, mask, valid, place, q, own, before, after)


def merge_kernel(count, kind_ref, base_ref, x_ref, out_ref, sems):
    heads = kind_ref.shape[0]
    size = out_ref.shape[1] // heads
    copies = []
    for s in range(count):
        start = pl.multiple_of(head_at(s, kind_ref, heads) * size, size)
        copy = pltpu.make_async_copy(
            x_ref.at[:, pl.ds(s * size, size)], out_ref.at[:, pl.ds(start, size)], sems.at[s]
        )
        copy.start()
        copies.append(copy)
    for copy in copies:
        copy.wait()


def merge(kind, base, x, count):
    return pl.pallas_call(
        functools.partial(merge_kernel, count),
        in_specs=[pl.BlockSpec(memory_space=pltpu.SMEM)]
        + [pl.BlockSpec(memory_space=pltpu.HBM), pl.BlockSpec(memory_space=pl.ANY)],
        out_specs=pl.BlockSpec(memory_space=pltpu.HBM),
        out_shape=jax.ShapeDtypeStruct(base.shape, BF),
        scratch_shapes=[pltpu.SemaphoreType.DMA((count,))],
        input_output_aliases={1: 0},
        compiler_params=params(),
        cost_estimate=pl.CostEstimate(flops=0, bytes_accessed=4 * x.size, transcendentals=0),
        name="merge_heads",
    )(kind, base, x)


def local(queries, keys, values, gain_q, gain_k, head_kind, tile_mask, frame_valid):
    heads = head_kind.shape[0]
    tokens, channels = queries.shape[1:]
    size = channels // heads
    tile = tokens // tile_mask.shape[1]
    frames = lax.axis_size("frames")
    blocks = lax.axis_size("heads")
    position = lax.axis_index("frames")
    scale = math.log2(math.e) / math.sqrt(size)
    share = tokens // frames
    q, k, v = queries[0], keys[0], values[0]

    parts = local_sums(q, k, blocks, tile)
    parts = lax.all_to_all(parts, "heads", split_axis=0, concat_axis=0, tiled=True)

    place = position[None]
    valid_row = frame_valid[None, :]
    up = [(i, i + 1) for i in range(frames - 1)]
    down = [(j, i) for i, j in up]

    def exchange(x):
        x = x.reshape(frames, share, x.shape[1])
        return lax.all_to_all(x, "frames", split_axis=0, concat_axis=0, tiled=True).reshape(
            tokens, x.shape[2]
        )

    def branch(count, late):
        rest = heads - count

        def run(q, k, v, parts):
            args = (head_kind, parts, gain_q, gain_k, q, k, v)

            def near():
                pair, near_q = pack(*args, (), count, rest, False, blocks * channels, tile)
                earlier = lax.ppermute(pair, "frames", up)
                later = lax.ppermute(pair, "frames", down)
                return near_q, pair, earlier, later

            def attend(near_q, pair, earlier, later):
                return spatial(
                    head_kind, tile_mask, frame_valid, place, near_q, pair, earlier, later,
                    count, rest, channels, scale, tile,
                )

            def send(*after):
                (sent,) = pack(*args, after, 0, count, True, blocks * channels, tile)
                return exchange(sent)

            if late == 0:
                mine = send()
                found = near()
                after = found[1:2]
            elif late == 1:
                found = near()
                mine = send(*found[2:])
                after = ()
            else:
                found = near()
                base = attend(*found)
                mine = send(base)
                after = ()
            told = temporal(mine, valid_row, after, count, share, size, scale)
            back = exchange(told)
            if late < 2:
                base = attend(*found)
            return merge(head_kind, base, back, count)

        return run

    count = jnp.sum(head_kind)
    odd = lax.axis_index("heads") % 2
    choice = count - 1 + jnp.where((odd == 1) & (count > 2), heads - 3, 0)
    branches = [branch(c, 0) for c in range(1, heads)]
    branches += [branch(c, 2) for c in range(3, heads)]
    out = lax.switch(choice, branches, q, k, v, parts)
    return out[None]


def solution(mesh):
    placed = (
        P("frames", None, "heads"),
        P("frames", None, "heads"),
        P("frames", None, "heads"),
        P("heads"),
        P("heads"),
        P("heads"),
        P("heads", None, None),
        P(),
    )
    return jax.shard_map(
        local, mesh=mesh, in_specs=placed, out_specs=P("frames", None, "heads"), check_vma=False
    )
```

```python
import functools
import math

import jax
import jax.numpy as jnp
from jax import lax
from jax.experimental import pallas as pl
from jax.experimental.pallas import tpu as pltpu
from jax.sharding import PartitionSpec as P

epsilon = 1e-06
VIDEO = 32
SHIFT = 8
LOW = -1e30
BF = jnp.bfloat16
F32 = jnp.float32


def params():
    return pltpu.CompilerParams(vmem_limit_bytes=40 * 1024 * 1024)


def head_at(slot, kind_ref, heads):
    flags = [kind_ref[h] for h in range(heads)]
    total = sum(flags)
    found = jnp.int32(0)
    seen = jnp.int32(0)
    for h in range(heads):
        rank = jnp.where(flags[h] > 0, seen, total + h - seen)
        found = jnp.where(rank == slot, h, found)
        seen = seen + flags[h]
    return found


def sums_kernel(groups, tile, q_ref, k_ref, out_ref, q_buf, k_buf, sems):
    tokens = q_ref.shape[0]
    steps = tokens // tile
    copies = []
    for i in range(steps):
        rows = pl.ds(i * tile, tile)
        for n, (ref, buf) in enumerate(((q_ref, q_buf), (k_ref, k_buf))):
            copy = pltpu.make_async_copy(ref.at[rows, :], buf.at[rows, :], sems.at[2 * i + n])
            copy.start()
            copies.append(copy)
    for i in range(steps):
        for n, buf in enumerate((q_buf, k_buf)):
            copies[2 * i + n].wait()
            x = buf[pl.ds(i * tile, tile), :].astype(F32)
            x = x * x
            part = x[:, :128]
            for g in range(1, groups):
                part = part + x[:, g * 128 : (g + 1) * 128]
            row = jnp.sum(part.T, axis=0, keepdims=True)
            at = n * steps + i
            out_ref[:, at : at + 1, :] = jnp.broadcast_to(row[None], (out_ref.shape[0], 1, tile))


def local_sums(q, k, copies, tile):
    tokens, channels = q.shape
    steps = tokens // tile
    return pl.pallas_call(
        functools.partial(sums_kernel, channels // 128, tile),
        in_specs=[pl.BlockSpec(memory_space=pl.ANY)] * 2,
        out_specs=pl.BlockSpec(memory_space=pltpu.VMEM),
        out_shape=jax.ShapeDtypeStruct((copies, 2 * steps, tile), F32),
        scratch_shapes=[pltpu.VMEM((tokens, channels), BF)] * 2
        + [pltpu.SemaphoreType.DMA((2 * steps,))],
        compiler_params=params(),
        cost_estimate=pl.CostEstimate(
            flops=4 * q.size, bytes_accessed=4 * q.size, transcendentals=0
        ),
        name="square_sums",
    )(*(pltpu.with_memory_space_constraint(x, pltpu.HBM) for x in (q, k)))


def stage_kernel(kind_ref, odd_ref, q_ref, k_ref, v_ref, staged_ref, choice_ref, sems):
    heads, _, width = staged_ref.shape
    size = width // 3

    def copies(s):
        columns = pl.ds(pl.multiple_of(head_at(s, kind_ref, heads) * size, size), size)
        return [
            pltpu.make_async_copy(
                ref.at[:, columns],
                staged_ref.at[s, :, pl.ds(n * size, size)],
                sems.at[3 * s + n],
            )
            for n, ref in enumerate((q_ref, k_ref, v_ref))
        ]

    def begin(s, carry):
        for copy in copies(s):
            copy.start()
        return carry

    def end(s, carry):
        for copy in copies(s):
            copy.wait()
        return carry

    lax.fori_loop(0, heads, begin, 0)
    count = sum(kind_ref[h] for h in range(heads))
    second = (odd_ref[0] == 1) & (count > 2)
    choice_ref[0] = count - 1 + jnp.where(second, heads - 3, 0)
    lax.fori_loop(0, heads, end, 0)


def stage(kind, odd, q, k, v):
    tokens, channels = q.shape
    heads = kind.shape[0]
    return pl.pallas_call(
        stage_kernel,
        in_specs=[pl.BlockSpec(memory_space=pltpu.SMEM)] * 2
        + [pl.BlockSpec(memory_space=pl.ANY)] * 3,
        out_specs=[
            pl.BlockSpec(memory_space=pltpu.VMEM),
            pl.BlockSpec(memory_space=pltpu.SMEM),
        ],
        out_shape=[
            pltpu.VMEM((heads, tokens, 3 * channels // heads), BF),
            jax.ShapeDtypeStruct((1,), jnp.int32),
        ],
        scratch_shapes=[pltpu.SemaphoreType.DMA((3 * heads,))],
        compiler_params=params(),
        cost_estimate=pl.CostEstimate(flops=0, bytes_accessed=12 * q.size, transcendentals=0),
        name="stage_heads",
    )(kind, odd, *(pltpu.with_memory_space_constraint(x, pltpu.HBM) for x in (q, k, v)))


def pack_kernel(
    all_channels, tile, first, count, joined, kind_ref, parts_ref, gq_ref, gk_ref, staged_ref, *rest
):
    if joined:
        out_ref, out_buf, rq, rk, out_sems = rest[-5:]
    else:
        out_ref, qn_ref, out_buf, rq, rk, out_sems = rest[-6:]
    heads, tokens, _ = staged_ref.shape
    width = out_buf.shape[2]
    size = staged_ref.shape[2] // 3
    total = jnp.sum(parts_ref[...], axis=0)
    scale = lax.rsqrt(total / all_channels + epsilon)
    rows = tokens // tile
    for c in range(rows):
        here = pl.ds(c * tile, tile)
        rq[here, :] = jnp.broadcast_to(scale[c : c + 1, :], (tile, tile)).T
        rk[here, :] = jnp.broadcast_to(scale[rows + c : rows + c + 1, :], (tile, tile)).T

    def store(s):
        columns = pl.ds(pl.multiple_of(s * width, width), width)
        return pltpu.make_async_copy(out_buf.at[s], out_ref.at[:, columns], out_sems.at[s])

    def work(s, carry):
        at = first + s
        start = pl.multiple_of(head_at(at, kind_ref, heads) * size, size)
        gain_q = gq_ref[pl.ds(start, size)].reshape(1, size)
        gain_k = gk_ref[pl.ds(start, size)].reshape(1, size)
        normed_q = (staged_ref[at, :, 0:size].astype(F32) * rq[...] * gain_q).astype(BF)
        normed_k = (staged_ref[at, :, size : 2 * size].astype(F32) * rk[...] * gain_k).astype(BF)
        if joined:
            out_buf[s, :, 0:size] = normed_q
        else:
            qn_ref[:, pl.ds(pl.multiple_of(s * size, size), size)] = normed_q
        out_buf[s, :, width - 2 * size : width - size] = normed_k
        out_buf[s, :, width - size : width] = staged_ref[at, :, 2 * size : 3 * size]
        store(s).start()
        return carry

    lax.fori_loop(0, count, work, 0)

    def end(s, carry):
        store(s).wait()
        return carry

    lax.fori_loop(0, count, end, 0)


def pack(kind, parts, gain_q, gain_k, staged, after, first, count, joined, all_channels, tile):
    _, tokens, wide = staged.shape
    size = wide // 3
    width = (3 if joined else 2) * size
    out_shape = [jax.ShapeDtypeStruct((tokens, count * width), BF)]
    out_specs = [pl.BlockSpec(memory_space=pl.ANY)]
    if joined:
        out_shape = [pltpu.HBM((tokens, count * width), BF)]
    if not joined:
        out_shape.append(jax.ShapeDtypeStruct((tokens, count * size), BF))
        out_specs.append(pl.BlockSpec(memory_space=pltpu.VMEM))
    return pl.pallas_call(
        functools.partial(pack_kernel, all_channels, tile, first, count, joined),
        in_specs=[pl.BlockSpec(memory_space=pltpu.SMEM)]
        + [pl.BlockSpec(memory_space=pltpu.VMEM)] * 4
        + [pl.BlockSpec(memory_space=pl.ANY)] * len(after),
        out_specs=out_specs,
        out_shape=out_shape,
        scratch_shapes=[
            pltpu.VMEM((count, tokens, width), BF),
            pltpu.VMEM((tokens, size), F32),
            pltpu.VMEM((tokens, size), F32),
            pltpu.SemaphoreType.DMA((count,)),
        ],
        compiler_params=params(),
        cost_estimate=pl.CostEstimate(
            flops=4 * tokens * size * count,
            bytes_accessed=12 * tokens * size * count,
            transcendentals=0,
        ),
        name="pack_temporal" if joined else "pack_spatial",
    )(kind, parts, gain_q, gain_k, staged, *after)


def video_rows(frames, share):
    spans = []
    start = 0
    while start < frames:
        stop = min(frames, ((start + SHIFT) // VIDEO + 1) * VIDEO - SHIFT)
        spans.append((start * share, stop * share))
        start = stop
    return spans


def temporal_kernel(scale, count, share, x_ref, valid_ref, *rest):
    spans = video_rows(valid_ref.shape[1], share)
    out_ref, x_buf, out_buf, live_buf, *masks = rest[-6 - len(spans) : -2]
    in_sems, out_sems = rest[-2:]
    rows = x_ref.shape[0]
    frames = valid_ref.shape[1]
    size = out_buf.shape[2]

    def load(s):
        columns = pl.ds(pl.multiple_of(s * 3 * size, 3 * size), 3 * size)
        return pltpu.make_async_copy(x_ref.at[:, columns], x_buf.at[s], in_sems.at[s])

    def begin(s, carry):
        load(s).start()
        return carry

    lax.fori_loop(0, count, begin, 0)
    bits = share.bit_length() - 1
    live = jnp.where(valid_ref[...] > 0, 1.0, 0.0).astype(F32)
    owner = lax.broadcasted_iota(jnp.int32, (rows, frames), 0) >> bits
    hot = jnp.where(owner == lax.broadcasted_iota(jnp.int32, (rows, frames), 1), 1.0, 0.0)
    hot = hot.astype(BF)
    over = (((1,), (1,)), ((), ()))
    live_row = lax.dot_general(
        jnp.broadcast_to(live, (8, frames)).astype(BF), hot, over, preferred_element_type=F32
    )
    live_buf[...] = lax.dot_general(
        hot, jnp.broadcast_to(live, (size, frames)).astype(BF), over, preferred_element_type=F32
    )
    for (low, high), mask in zip(spans, masks):
        n = high - low
        at_row = lax.broadcasted_iota(jnp.int32, (n, n), 0)
        at_col = lax.broadcasted_iota(jnp.int32, (n, n), 1)
        same_token = ((at_row ^ at_col) & (share - 1)) == 0
        allowed = same_token & ((live_row[0:1, low:high] > 0.5) | (at_row == at_col))
        mask[...] = jnp.where(allowed, 0.0, LOW).astype(F32)

    def store(s):
        columns = pl.ds(pl.multiple_of(s * size, size), size)
        return pltpu.make_async_copy(out_buf.at[s], out_ref.at[:, columns], out_sems.at[s])

    for s in range(count):
        load(s).wait()
    for s in range(count):
        for (low, high), mask in zip(spans, masks):
            here = pl.ds(low, high - low)
            x = lax.dot_general(
                x_buf[s, here, 0:size],
                x_buf[s, here, size : 2 * size],
                over,
                preferred_element_type=F32,
            )
            x = x + mask[...]
            p = jnp.exp2((x - jnp.max(x, axis=1, keepdims=True)) * scale)
            total = jnp.sum(p, axis=1, keepdims=True)
            o = jnp.dot(
                p.astype(BF), x_buf[s, here, 2 * size : 3 * size], preferred_element_type=F32
            )
            out_buf[s, here, :] = (o / total * live_buf[here, :]).astype(BF)
        store(s).start()

    def end(s, carry):
        store(s).wait()
        return carry

    lax.fori_loop(0, count, end, 0)


def temporal(x, valid_row, after, count, share, size, scale):
    rows = x.shape[0]
    return pl.pallas_call(
        functools.partial(temporal_kernel, scale, count, share),
        in_specs=[
            pl.BlockSpec(memory_space=pl.ANY),
            pl.BlockSpec(memory_space=pltpu.VMEM),
        ]
        + [pl.BlockSpec(memory_space=pl.ANY)] * len(after),
        out_specs=pl.BlockSpec(memory_space=pl.ANY),
        out_shape=jax.ShapeDtypeStruct((rows, count * size), BF),
        scratch_shapes=[
            pltpu.VMEM((count, rows, 3 * size), BF),
            pltpu.VMEM((count, rows, size), BF),
            pltpu.VMEM((rows, size), F32),
            *[
                pltpu.VMEM((high - low, high - low), F32)
                for low, high in video_rows(valid_row.shape[1], share)
            ],
            pltpu.SemaphoreType.DMA((count,)),
            pltpu.SemaphoreType.DMA((count,)),
        ],
        compiler_params=params(),
        cost_estimate=pl.CostEstimate(
            flops=4 * rows * rows * size * count,
            bytes_accessed=8 * rows * size * count,
            transcendentals=rows * rows * count,
        ),
        name="temporal_heads",
    )(x, valid_row, *after)


def spatial_kernel(
    scale, tile, first, kind_ref, mask_ref, valid_ref, place_ref,
    q_ref, own_ref, before_ref, after_ref, out_ref
):
    heads = kind_ref.shape[0]
    head = head_at(first + pl.program_id(0), kind_ref, heads)
    tiles = own_ref.shape[0] // tile
    i = pl.program_id(1)
    frames = (before_ref, own_ref, after_ref)
    place = place_ref[0]
    last = valid_ref.shape[0] - 1
    near = [None, jnp.bool_(True), None]
    for o, there in ((0, jnp.maximum(place - 1, 0)), (2, jnp.minimum(place + 1, last))):
        same = ((there + SHIFT) // VIDEO == (place + SHIFT) // VIDEO) & (there != place)
        near[o] = same & (valid_ref[there] > 0)
    own_live = jnp.where(valid_ref[place] > 0, 1.0, 0.0).astype(F32)
    q = q_ref[...]
    pieces = []
    for o in range(3):
        s = lax.dot_general(
            q, frames[o][:, 0:128], (((1,), (1,)), ((), ())), preferred_element_type=F32
        )
        for j in range(tiles):
            ok = (mask_ref[head, i, o * tiles + j] > 0) & near[o]
            low = jnp.where(ok, 0.0, LOW).astype(F32)
            pieces.append(s[:, j * tile : (j + 1) * tile] + low)
    top = pieces[0]
    for x in pieces[1:]:
        top = jnp.maximum(top, x)
    top = jnp.max(top, axis=1, keepdims=True)
    pieces = [jnp.exp2((x - top) * scale) for x in pieces]
    total = pieces[0]
    for x in pieces[1:]:
        total = total + x
    total = jnp.sum(total, axis=1, keepdims=True)
    o_sum = None
    for o in range(3):
        p = jnp.concatenate([x.astype(BF) for x in pieces[o * tiles : (o + 1) * tiles]], axis=1)
        part = jnp.dot(p, frames[o][:, 128:256], preferred_element_type=F32)
        o_sum = part if o_sum is None else o_sum + part
    out_ref[...] = (o_sum / total * own_live).astype(BF)


def spatial(kind, mask, valid, place, q, own, before, after, first, count, channels, scale, tile):
    tokens = q.shape[0]
    heads = kind.shape[0]
    size = channels // heads

    def slot(i, j, *_):
        return (0, i)

    return pl.pallas_call(
        functools.partial(spatial_kernel, scale, tile, first),
        grid_spec=pltpu.PrefetchScalarGridSpec(
            num_scalar_prefetch=4,
            grid=(count, tokens // tile),
            in_specs=[pl.BlockSpec((tile, size), lambda i, j, *_: (j, i))]
            + [pl.BlockSpec((tokens, 2 * size), slot)] * 3,
            out_specs=pl.BlockSpec(
                (tile, size),
                lambda i, j, kind_ref, *_: (j, head_at(first + i, kind_ref, heads)),
            ),
        ),
        out_shape=jax.ShapeDtypeStruct((tokens, channels), BF),
        compiler_params=params(),
        cost_estimate=pl.CostEstimate(
            flops=12 * tokens * tokens * size * count,
            bytes_accessed=16 * tokens * size * count,
            transcendentals=3 * tokens * tokens * count,
        ),
        name="spatial_heads",
    )(kind, mask, valid, place, q, own, before, after)


def merge_kernel(count, kind_ref, base_ref, x_ref, out_ref, sems):
    heads = kind_ref.shape[0]
    size = out_ref.shape[1] // heads
    copies = []
    for s in range(count):
        start = pl.multiple_of(head_at(s, kind_ref, heads) * size, size)
        copy = pltpu.make_async_copy(
            x_ref.at[:, pl.ds(s * size, size)], out_ref.at[:, pl.ds(start, size)], sems.at[s]
        )
        copy.start()
        copies.append(copy)
    for copy in copies:
        copy.wait()


def merge(kind, base, x, count):
    return pl.pallas_call(
        functools.partial(merge_kernel, count),
        in_specs=[pl.BlockSpec(memory_space=pltpu.SMEM)]
        + [pl.BlockSpec(memory_space=pltpu.HBM), pl.BlockSpec(memory_space=pl.ANY)],
        out_specs=pl.BlockSpec(memory_space=pltpu.HBM),
        out_shape=jax.ShapeDtypeStruct(base.shape, BF),
        scratch_shapes=[pltpu.SemaphoreType.DMA((count,))],
        input_output_aliases={1: 0},
        compiler_params=params(),
        cost_estimate=pl.CostEstimate(flops=0, bytes_accessed=4 * x.size, transcendentals=0),
        name="merge_heads",
    )(kind, base, x)


def local(queries, keys, values, gain_q, gain_k, head_kind, tile_mask, frame_valid):
    heads = head_kind.shape[0]
    tokens, channels = queries.shape[1:]
    size = channels // heads
    tile = tokens // tile_mask.shape[1]
    frames = lax.axis_size("frames")
    blocks = lax.axis_size("heads")
    position = lax.axis_index("frames")
    scale = math.log2(math.e) / math.sqrt(size)
    share = tokens // frames
    q, k, v = queries[0], keys[0], values[0]

    odd = lax.axis_index("heads") % 2
    parts = local_sums(q, k, blocks, tile)
    staged, choice = stage(head_kind, odd[None], q, k, v)
    parts = lax.all_to_all(parts, "heads", split_axis=0, concat_axis=0, tiled=True)

    place = position[None]
    valid_row = frame_valid[None, :]
    up = [(i, i + 1) for i in range(frames - 1)]
    down = [(j, i) for i, j in up]

    def exchange(x):
        x = x.reshape(frames, share, x.shape[1])
        return lax.all_to_all(x, "frames", split_axis=0, concat_axis=0, tiled=True).reshape(
            tokens, x.shape[2]
        )

    def branch(count, late):
        rest = heads - count

        def run(staged, parts):
            args = (head_kind, parts, gain_q, gain_k, staged)

            def near():
                pair, near_q = pack(*args, (), count, rest, False, blocks * channels, tile)
                earlier = lax.ppermute(pair, "frames", up)
                later = lax.ppermute(pair, "frames", down)
                return near_q, pair, earlier, later

            def attend(near_q, pair, earlier, later):
                return spatial(
                    head_kind, tile_mask, frame_valid, place, near_q, pair, earlier, later,
                    count, rest, channels, scale, tile,
                )

            def send(*after):
                (sent,) = pack(*args, after, 0, count, True, blocks * channels, tile)
                return exchange(sent)

            if late == 0:
                mine = send()
                found = near()
                after = found[1:2]
            elif late == 1:
                found = near()
                mine = send(*found[2:])
                after = ()
            else:
                found = near()
                base = attend(*found)
                mine = send(base)
                after = ()
            told = temporal(mine, valid_row, after, count, share, size, scale)
            back = exchange(told)
            if late < 2:
                base = attend(*found)
            return merge(head_kind, base, back, count)

        return run

    branches = [branch(c, 0) for c in range(1, heads)]
    branches += [branch(c, 2) for c in range(3, heads)]
    out = lax.switch(choice[0], branches, staged, parts)
    return out[None]


def solution(mesh):
    placed = (
        P("frames", None, "heads"),
        P("frames", None, "heads"),
        P("frames", None, "heads"),
        P("heads"),
        P("heads"),
        P("heads"),
        P("heads", None, None),
        P(),
    )
    return jax.shard_map(
        local, mesh=mesh, in_specs=placed, out_specs=P("frames", None, "heads"), check_vma=False
    )
```

```python
import functools
import math

import jax
import jax.numpy as jnp
from jax import lax
from jax.experimental import pallas as pl
from jax.experimental.pallas import tpu as pltpu
from jax.sharding import PartitionSpec as P

epsilon = 1e-06
VIDEO = 32
SHIFT = 8
LOW = -1e30
BF = jnp.bfloat16
F32 = jnp.float32


def params():
    return pltpu.CompilerParams(vmem_limit_bytes=40 * 1024 * 1024)


def head_at(slot, kind_ref, heads):
    flags = [kind_ref[h] for h in range(heads)]
    total = sum(flags)
    found = jnp.int32(0)
    seen = jnp.int32(0)
    for h in range(heads):
        rank = jnp.where(flags[h] > 0, seen, total + h - seen)
        found = jnp.where(rank == slot, h, found)
        seen = seen + flags[h]
    return found


def sums_kernel(groups, tile, q_ref, k_ref, out_ref, q_buf, k_buf, sems):
    tokens = q_ref.shape[0]
    steps = tokens // tile
    copies = []
    for i in range(steps):
        rows = pl.ds(i * tile, tile)
        for n, (ref, buf) in enumerate(((q_ref, q_buf), (k_ref, k_buf))):
            copy = pltpu.make_async_copy(ref.at[rows, :], buf.at[rows, :], sems.at[2 * i + n])
            copy.start()
            copies.append(copy)
    for i in range(steps):
        for n, buf in enumerate((q_buf, k_buf)):
            copies[2 * i + n].wait()
            x = buf[pl.ds(i * tile, tile), :].astype(F32)
            x = x * x
            part = x[:, :128]
            for g in range(1, groups):
                part = part + x[:, g * 128 : (g + 1) * 128]
            row = jnp.sum(part.T, axis=0, keepdims=True)
            at = n * steps + i
            out_ref[:, at : at + 1, :] = jnp.broadcast_to(row[None], (out_ref.shape[0], 1, tile))


def local_sums(q, k, copies, tile):
    tokens, channels = q.shape
    steps = tokens // tile
    return pl.pallas_call(
        functools.partial(sums_kernel, channels // 128, tile),
        in_specs=[pl.BlockSpec(memory_space=pl.ANY)] * 2,
        out_specs=pl.BlockSpec(memory_space=pltpu.VMEM),
        out_shape=jax.ShapeDtypeStruct((copies, 2 * steps, tile), F32),
        scratch_shapes=[pltpu.VMEM((tokens, channels), BF)] * 2
        + [pltpu.SemaphoreType.DMA((2 * steps,))],
        compiler_params=params(),
        cost_estimate=pl.CostEstimate(
            flops=4 * q.size, bytes_accessed=4 * q.size, transcendentals=0
        ),
        name="square_sums",
    )(*(pltpu.with_memory_space_constraint(x, pltpu.HBM) for x in (q, k)))


def stage_kernel(kind_ref, odd_ref, q_ref, k_ref, v_ref, staged_ref, choice_ref, sems):
    heads, _, width = staged_ref.shape
    size = width // 3

    def copies(s):
        columns = pl.ds(pl.multiple_of(head_at(s, kind_ref, heads) * size, size), size)
        return [
            pltpu.make_async_copy(
                ref.at[:, columns],
                staged_ref.at[s, :, pl.ds(n * size, size)],
                sems.at[3 * s + n],
            )
            for n, ref in enumerate((q_ref, k_ref, v_ref))
        ]

    def begin(s, carry):
        for copy in copies(s):
            copy.start()
        return carry

    def end(s, carry):
        for copy in copies(s):
            copy.wait()
        return carry

    lax.fori_loop(0, heads, begin, 0)
    count = sum(kind_ref[h] for h in range(heads))
    second = (odd_ref[0] == 1) & (count > 2)
    choice_ref[0] = count - 1 + jnp.where(second, heads - 3, 0)
    lax.fori_loop(0, heads, end, 0)


def stage(kind, odd, q, k, v):
    tokens, channels = q.shape
    heads = kind.shape[0]
    return pl.pallas_call(
        stage_kernel,
        in_specs=[pl.BlockSpec(memory_space=pltpu.SMEM)] * 2
        + [pl.BlockSpec(memory_space=pl.ANY)] * 3,
        out_specs=[
            pl.BlockSpec(memory_space=pltpu.VMEM),
            pl.BlockSpec(memory_space=pltpu.SMEM),
        ],
        out_shape=[
            pltpu.VMEM((heads, tokens, 3 * channels // heads), BF),
            jax.ShapeDtypeStruct((1,), jnp.int32),
        ],
        scratch_shapes=[pltpu.SemaphoreType.DMA((3 * heads,))],
        compiler_params=params(),
        cost_estimate=pl.CostEstimate(flops=0, bytes_accessed=12 * q.size, transcendentals=0),
        name="stage_heads",
    )(kind, odd, *(pltpu.with_memory_space_constraint(x, pltpu.HBM) for x in (q, k, v)))


def pack_kernel(
    all_channels, tile, first, count, joined, kind_ref, parts_ref, gq_ref, gk_ref, staged_ref, *rest
):
    if joined:
        out_ref, out_buf, rq, rk, out_sems = rest[-5:]
    else:
        out_ref, qn_ref, out_buf, rq, rk, out_sems = rest[-6:]
    heads, tokens, _ = staged_ref.shape
    width = out_buf.shape[2]
    size = staged_ref.shape[2] // 3
    total = jnp.sum(parts_ref[...], axis=0)
    scale = lax.rsqrt(total / all_channels + epsilon)
    rows = tokens // tile
    for c in range(rows):
        here = pl.ds(c * tile, tile)
        rq[here, :] = jnp.broadcast_to(scale[c : c + 1, :], (tile, tile)).T
        rk[here, :] = jnp.broadcast_to(scale[rows + c : rows + c + 1, :], (tile, tile)).T

    def store(s):
        columns = pl.ds(pl.multiple_of(s * width, width), width)
        return pltpu.make_async_copy(out_buf.at[s], out_ref.at[:, columns], out_sems.at[s])

    def work(s, carry):
        at = first + s
        start = pl.multiple_of(head_at(at, kind_ref, heads) * size, size)
        gain_q = gq_ref[pl.ds(start, size)].reshape(1, size)
        gain_k = gk_ref[pl.ds(start, size)].reshape(1, size)
        normed_q = (staged_ref[at, :, 0:size].astype(F32) * rq[...] * gain_q).astype(BF)
        normed_k = (staged_ref[at, :, size : 2 * size].astype(F32) * rk[...] * gain_k).astype(BF)
        if joined:
            out_buf[s, :, 0:size] = normed_q
        else:
            qn_ref[:, pl.ds(pl.multiple_of(s * size, size), size)] = normed_q
        out_buf[s, :, width - 2 * size : width - size] = normed_k
        out_buf[s, :, width - size : width] = staged_ref[at, :, 2 * size : 3 * size]
        store(s).start()
        return carry

    lax.fori_loop(0, count, work, 0)

    def end(s, carry):
        store(s).wait()
        return carry

    lax.fori_loop(0, count, end, 0)


def pack(kind, parts, gain_q, gain_k, staged, after, first, count, joined, all_channels, tile):
    _, tokens, wide = staged.shape
    size = wide // 3
    width = (3 if joined else 2) * size
    out_shape = [jax.ShapeDtypeStruct((tokens, count * width), BF)]
    out_specs = [pl.BlockSpec(memory_space=pl.ANY)]
    if joined:
        out_shape = [pltpu.HBM((tokens, count * width), BF)]
    if not joined:
        out_shape.append(jax.ShapeDtypeStruct((tokens, count * size), BF))
        out_specs.append(pl.BlockSpec(memory_space=pltpu.VMEM))
    return pl.pallas_call(
        functools.partial(pack_kernel, all_channels, tile, first, count, joined),
        in_specs=[pl.BlockSpec(memory_space=pltpu.SMEM)]
        + [pl.BlockSpec(memory_space=pltpu.VMEM)] * 4
        + [pl.BlockSpec(memory_space=pl.ANY)] * len(after),
        out_specs=out_specs,
        out_shape=out_shape,
        scratch_shapes=[
            pltpu.VMEM((count, tokens, width), BF),
            pltpu.VMEM((tokens, size), F32),
            pltpu.VMEM((tokens, size), F32),
            pltpu.SemaphoreType.DMA((count,)),
        ],
        compiler_params=params(),
        cost_estimate=pl.CostEstimate(
            flops=4 * tokens * size * count,
            bytes_accessed=12 * tokens * size * count,
            transcendentals=0,
        ),
        name="pack_temporal" if joined else "pack_spatial",
    )(kind, parts, gain_q, gain_k, staged, *after)


def video_rows(frames, share):
    spans = []
    start = 0
    while start < frames:
        stop = min(frames, ((start + SHIFT) // VIDEO + 1) * VIDEO - SHIFT)
        spans.append((start * share, stop * share))
        start = stop
    return spans


def temporal_kernel(scale, count, share, x_ref, valid_ref, *rest):
    spans = video_rows(valid_ref.shape[1], share)
    out_ref, x_buf, out_buf, live_buf, *masks = rest[-6 - len(spans) : -2]
    in_sems, out_sems = rest[-2:]
    rows = x_ref.shape[0]
    frames = valid_ref.shape[1]
    size = out_buf.shape[2]

    def load(s):
        columns = pl.ds(pl.multiple_of(s * 3 * size, 3 * size), 3 * size)
        return pltpu.make_async_copy(x_ref.at[:, columns], x_buf.at[s], in_sems.at[s])

    def begin(s, carry):
        load(s).start()
        return carry

    lax.fori_loop(0, count, begin, 0)
    bits = share.bit_length() - 1
    live = jnp.where(valid_ref[...] > 0, 1.0, 0.0).astype(F32)
    owner = lax.broadcasted_iota(jnp.int32, (rows, frames), 0) >> bits
    hot = jnp.where(owner == lax.broadcasted_iota(jnp.int32, (rows, frames), 1), 1.0, 0.0)
    hot = hot.astype(BF)
    over = (((1,), (1,)), ((), ()))
    live_row = lax.dot_general(
        jnp.broadcast_to(live, (8, frames)).astype(BF), hot, over, preferred_element_type=F32
    )
    live_buf[...] = lax.dot_general(
        hot, jnp.broadcast_to(live, (size, frames)).astype(BF), over, preferred_element_type=F32
    )
    for (low, high), mask in zip(spans, masks):
        n = high - low
        at_row = lax.broadcasted_iota(jnp.int32, (n, n), 0)
        at_col = lax.broadcasted_iota(jnp.int32, (n, n), 1)
        same_token = ((at_row ^ at_col) & (share - 1)) == 0
        allowed = same_token & ((live_row[0:1, low:high] > 0.5) | (at_row == at_col))
        mask[...] = jnp.where(allowed, 0.0, LOW).astype(F32)

    def store(s):
        columns = pl.ds(pl.multiple_of(s * size, size), size)
        return pltpu.make_async_copy(out_buf.at[s], out_ref.at[:, columns], out_sems.at[s])

    for s in range(count):
        load(s).wait()
    for s in range(count):
        for (low, high), mask in zip(spans, masks):
            here = pl.ds(low, high - low)
            x = lax.dot_general(
                x_buf[s, here, 0:size],
                x_buf[s, here, size : 2 * size],
                over,
                preferred_element_type=F32,
            )
            x = x + mask[...]
            p = jnp.exp2((x - jnp.max(x, axis=1, keepdims=True)) * scale)
            total = jnp.sum(p, axis=1, keepdims=True)
            o = jnp.dot(
                p.astype(BF), x_buf[s, here, 2 * size : 3 * size], preferred_element_type=F32
            )
            out_buf[s, here, :] = (o / total * live_buf[here, :]).astype(BF)
        store(s).start()

    def end(s, carry):
        store(s).wait()
        return carry

    lax.fori_loop(0, count, end, 0)


def temporal(x, valid_row, after, count, share, size, scale):
    rows = x.shape[0]
    return pl.pallas_call(
        functools.partial(temporal_kernel, scale, count, share),
        in_specs=[
            pl.BlockSpec(memory_space=pl.ANY),
            pl.BlockSpec(memory_space=pltpu.VMEM),
        ]
        + [pl.BlockSpec(memory_space=pl.ANY)] * len(after),
        out_specs=pl.BlockSpec(memory_space=pl.ANY),
        out_shape=jax.ShapeDtypeStruct((rows, count * size), BF),
        scratch_shapes=[
            pltpu.VMEM((count, rows, 3 * size), BF),
            pltpu.VMEM((count, rows, size), BF),
            pltpu.VMEM((rows, size), F32),
            *[
                pltpu.VMEM((high - low, high - low), F32)
                for low, high in video_rows(valid_row.shape[1], share)
            ],
            pltpu.SemaphoreType.DMA((count,)),
            pltpu.SemaphoreType.DMA((count,)),
        ],
        compiler_params=params(),
        cost_estimate=pl.CostEstimate(
            flops=4 * rows * rows * size * count,
            bytes_accessed=8 * rows * size * count,
            transcendentals=rows * rows * count,
        ),
        name="temporal_heads",
    )(x, valid_row, *after)


def spatial_kernel(
    scale, tile, first, kind_ref, mask_ref, valid_ref, place_ref,
    q_ref, own_ref, before_ref, after_ref, out_ref
):
    heads = kind_ref.shape[0]
    head = head_at(first + pl.program_id(0), kind_ref, heads)
    tiles = own_ref.shape[0] // tile
    frames = (before_ref, own_ref, after_ref)
    place = place_ref[0]
    last = valid_ref.shape[0] - 1
    near = [None, jnp.bool_(True), None]
    for o, there in ((0, jnp.maximum(place - 1, 0)), (2, jnp.minimum(place + 1, last))):
        same = ((there + SHIFT) // VIDEO == (place + SHIFT) // VIDEO) & (there != place)
        near[o] = same & (valid_ref[there] > 0)
    own_live = jnp.where(valid_ref[place] > 0, 1.0, 0.0).astype(F32)
    parts = q_ref.shape[0] // tile
    for sub in range(parts):
        i = pl.program_id(1) * parts + sub
        rows = pl.ds(sub * tile, tile)
        q = q_ref[rows, :]
        pieces = []
        for o in range(3):
            s = lax.dot_general(
                q, frames[o][:, 0:128], (((1,), (1,)), ((), ())), preferred_element_type=F32
            )
            for j in range(tiles):
                ok = (mask_ref[head, i, o * tiles + j] > 0) & near[o]
                low = jnp.where(ok, 0.0, LOW).astype(F32)
                pieces.append(s[:, j * tile : (j + 1) * tile] + low)
        top = pieces[0]
        for x in pieces[1:]:
            top = jnp.maximum(top, x)
        top = jnp.max(top, axis=1, keepdims=True)
        pieces = [jnp.exp2((x - top) * scale) for x in pieces]
        total = pieces[0]
        for x in pieces[1:]:
            total = total + x
        total = jnp.sum(total, axis=1, keepdims=True)
        o_sum = None
        for o in range(3):
            p = jnp.concatenate([x.astype(BF) for x in pieces[o * tiles : (o + 1) * tiles]], axis=1)
            part = jnp.dot(p, frames[o][:, 128:256], preferred_element_type=F32)
            o_sum = part if o_sum is None else o_sum + part
        out_ref[rows, :] = (o_sum / total * own_live).astype(BF)


def spatial(
    kind, mask, valid, place, q, own, before, after, first, count, channels, scale, tile, step
):
    tokens = q.shape[0]
    heads = kind.shape[0]
    size = channels // heads

    def slot(i, j, *_):
        return (0, i)

    return pl.pallas_call(
        functools.partial(spatial_kernel, scale, tile, first),
        grid_spec=pltpu.PrefetchScalarGridSpec(
            num_scalar_prefetch=4,
            grid=(count, tokens // step),
            in_specs=[pl.BlockSpec((step, size), lambda i, j, *_: (j, i))]
            + [pl.BlockSpec((tokens, 2 * size), slot)] * 3,
            out_specs=pl.BlockSpec(
                (step, size),
                lambda i, j, kind_ref, *_: (j, head_at(first + i, kind_ref, heads)),
            ),
        ),
        out_shape=jax.ShapeDtypeStruct((tokens, channels), BF),
        compiler_params=params(),
        cost_estimate=pl.CostEstimate(
            flops=12 * tokens * tokens * size * count,
            bytes_accessed=16 * tokens * size * count,
            transcendentals=3 * tokens * tokens * count,
        ),
        name="spatial_heads",
    )(kind, mask, valid, place, q, own, before, after)


def merge_kernel(count, kind_ref, base_ref, x_ref, out_ref, sems):
    heads = kind_ref.shape[0]
    size = out_ref.shape[1] // heads
    copies = []
    for s in range(count):
        start = pl.multiple_of(head_at(s, kind_ref, heads) * size, size)
        copy = pltpu.make_async_copy(
            x_ref.at[:, pl.ds(s * size, size)], out_ref.at[:, pl.ds(start, size)], sems.at[s]
        )
        copy.start()
        copies.append(copy)
    for copy in copies:
        copy.wait()


def merge(kind, base, x, count):
    return pl.pallas_call(
        functools.partial(merge_kernel, count),
        in_specs=[pl.BlockSpec(memory_space=pltpu.SMEM)]
        + [pl.BlockSpec(memory_space=pltpu.HBM), pl.BlockSpec(memory_space=pl.ANY)],
        out_specs=pl.BlockSpec(memory_space=pltpu.HBM),
        out_shape=jax.ShapeDtypeStruct(base.shape, BF),
        scratch_shapes=[pltpu.SemaphoreType.DMA((count,))],
        input_output_aliases={1: 0},
        compiler_params=params(),
        cost_estimate=pl.CostEstimate(flops=0, bytes_accessed=4 * x.size, transcendentals=0),
        name="merge_heads",
    )(kind, base, x)


def local(queries, keys, values, gain_q, gain_k, head_kind, tile_mask, frame_valid):
    heads = head_kind.shape[0]
    tokens, channels = queries.shape[1:]
    size = channels // heads
    tile = tokens // tile_mask.shape[1]
    frames = lax.axis_size("frames")
    blocks = lax.axis_size("heads")
    position = lax.axis_index("frames")
    scale = math.log2(math.e) / math.sqrt(size)
    share = tokens // frames
    q, k, v = queries[0], keys[0], values[0]

    odd = lax.axis_index("heads") % 2
    parts = local_sums(q, k, blocks, tile)
    staged, choice = stage(head_kind, odd[None], q, k, v)
    parts = lax.all_to_all(parts, "heads", split_axis=0, concat_axis=0, tiled=True)

    place = position[None]
    valid_row = frame_valid[None, :]
    up = [(i, i + 1) for i in range(frames - 1)]
    down = [(j, i) for i, j in up]

    def exchange(x):
        x = x.reshape(frames, share, x.shape[1])
        return lax.all_to_all(x, "frames", split_axis=0, concat_axis=0, tiled=True).reshape(
            tokens, x.shape[2]
        )

    def branch(count, late):
        rest = heads - count

        def run(staged, parts):
            args = (head_kind, parts, gain_q, gain_k, staged)

            def near():
                pair, near_q = pack(*args, (), count, rest, False, blocks * channels, tile)
                earlier = lax.ppermute(pair, "frames", up)
                later = lax.ppermute(pair, "frames", down)
                return near_q, pair, earlier, later

            def attend(near_q, pair, earlier, later):
                return spatial(
                    head_kind, tile_mask, frame_valid, place, near_q, pair, earlier, later,
                    count, rest, channels, scale, tile, tile if late == 2 else 2 * tile,
                )

            def send(*after):
                (sent,) = pack(*args, after, 0, count, True, blocks * channels, tile)
                return exchange(sent)

            if late == 0:
                mine = send()
                found = near()
                after = found[1:2]
            elif late == 1:
                found = near()
                mine = send(*found[2:])
                after = ()
            else:
                found = near()
                base = attend(*found)
                mine = send(base)
                after = ()
            told = temporal(mine, valid_row, after, count, share, size, scale)
            back = exchange(told)
            if late < 2:
                base = attend(*found)
            return merge(head_kind, base, back, count)

        return run

    branches = [branch(c, 0) for c in range(1, heads)]
    branches += [branch(c, 2) for c in range(3, heads)]
    out = lax.switch(choice[0], branches, staged, parts)
    return out[None]


def solution(mesh):
    placed = (
        P("frames", None, "heads"),
        P("frames", None, "heads"),
        P("frames", None, "heads"),
        P("heads"),
        P("heads"),
        P("heads"),
        P("heads", None, None),
        P(),
    )
    return jax.shard_map(
        local, mesh=mesh, in_specs=placed, out_specs=P("frames", None, "heads"), check_vma=False
    )
```

```python
import functools
import math

import jax
import jax.numpy as jnp
from jax import lax
from jax.experimental import pallas as pl
from jax.experimental.pallas import tpu as pltpu
from jax.sharding import PartitionSpec as P

epsilon = 1e-06
VIDEO = 32
SHIFT = 8
LOW = -1e30
BF = jnp.bfloat16
F32 = jnp.float32


def params():
    return pltpu.CompilerParams(vmem_limit_bytes=40 * 1024 * 1024)


def head_at(slot, kind_ref, heads):
    flags = [kind_ref[h] for h in range(heads)]
    total = sum(flags)
    found = jnp.int32(0)
    seen = jnp.int32(0)
    for h in range(heads):
        rank = jnp.where(flags[h] > 0, seen, total + h - seen)
        found = jnp.where(rank == slot, h, found)
        seen = seen + flags[h]
    return found


def sums_kernel(groups, tile, q_ref, k_ref, out_ref, q_buf, k_buf, sems):
    tokens = q_ref.shape[0]
    steps = tokens // tile
    copies = []
    for i in range(steps):
        rows = pl.ds(i * tile, tile)
        for n, (ref, buf) in enumerate(((q_ref, q_buf), (k_ref, k_buf))):
            copy = pltpu.make_async_copy(ref.at[rows, :], buf.at[rows, :], sems.at[2 * i + n])
            copy.start()
            copies.append(copy)
    for i in range(steps):
        for n, buf in enumerate((q_buf, k_buf)):
            copies[2 * i + n].wait()
            x = buf[pl.ds(i * tile, tile), :].astype(F32)
            x = x * x
            part = x[:, :128]
            for g in range(1, groups):
                part = part + x[:, g * 128 : (g + 1) * 128]
            row = jnp.sum(part.T, axis=0, keepdims=True)
            at = n * steps + i
            out_ref[:, at : at + 1, :] = jnp.broadcast_to(row[None], (out_ref.shape[0], 1, tile))


def local_sums(q, k, copies, tile):
    tokens, channels = q.shape
    steps = tokens // tile
    return pl.pallas_call(
        functools.partial(sums_kernel, channels // 128, tile),
        in_specs=[pl.BlockSpec(memory_space=pl.ANY)] * 2,
        out_specs=pl.BlockSpec(memory_space=pltpu.VMEM),
        out_shape=jax.ShapeDtypeStruct((copies, 2 * steps, tile), F32),
        scratch_shapes=[pltpu.VMEM((tokens, channels), BF)] * 2
        + [pltpu.SemaphoreType.DMA((2 * steps,))],
        compiler_params=params(),
        cost_estimate=pl.CostEstimate(
            flops=4 * q.size, bytes_accessed=4 * q.size, transcendentals=0
        ),
        name="square_sums",
    )(*(pltpu.with_memory_space_constraint(x, pltpu.HBM) for x in (q, k)))


def stage_kernel(kind_ref, odd_ref, q_ref, k_ref, v_ref, staged_ref, choice_ref, sems):
    heads, _, width = staged_ref.shape
    size = width // 3

    def copies(s):
        columns = pl.ds(pl.multiple_of(head_at(s, kind_ref, heads) * size, size), size)
        return [
            pltpu.make_async_copy(
                ref.at[:, columns],
                staged_ref.at[s, :, pl.ds(n * size, size)],
                sems.at[3 * s + n],
            )
            for n, ref in enumerate((q_ref, k_ref, v_ref))
        ]

    def begin(s, carry):
        for copy in copies(s):
            copy.start()
        return carry

    def end(s, carry):
        for copy in copies(s):
            copy.wait()
        return carry

    lax.fori_loop(0, heads, begin, 0)
    count = sum(kind_ref[h] for h in range(heads))
    second = (odd_ref[0] == 1) & (count > 2)
    choice_ref[0] = count - 1 + jnp.where(second, heads - 3, 0)
    lax.fori_loop(0, heads, end, 0)


def stage(kind, odd, q, k, v):
    tokens, channels = q.shape
    heads = kind.shape[0]
    return pl.pallas_call(
        stage_kernel,
        in_specs=[pl.BlockSpec(memory_space=pltpu.SMEM)] * 2
        + [pl.BlockSpec(memory_space=pl.ANY)] * 3,
        out_specs=[
            pl.BlockSpec(memory_space=pltpu.VMEM),
            pl.BlockSpec(memory_space=pltpu.SMEM),
        ],
        out_shape=[
            pltpu.VMEM((heads, tokens, 3 * channels // heads), BF),
            jax.ShapeDtypeStruct((1,), jnp.int32),
        ],
        scratch_shapes=[pltpu.SemaphoreType.DMA((3 * heads,))],
        compiler_params=params(),
        cost_estimate=pl.CostEstimate(flops=0, bytes_accessed=12 * q.size, transcendentals=0),
        name="stage_heads",
    )(kind, odd, *(pltpu.with_memory_space_constraint(x, pltpu.HBM) for x in (q, k, v)))


def pack_kernel(
    all_channels, tile, first, count, joined, kind_ref, parts_ref, gq_ref, gk_ref, staged_ref, *rest
):
    if joined:
        out_ref, out_buf, rq, rk, out_sems = rest[-5:]
    else:
        out_ref, qn_ref, out_buf, rq, rk, out_sems = rest[-6:]
    heads, tokens, _ = staged_ref.shape
    width = out_buf.shape[2]
    size = staged_ref.shape[2] // 3
    total = jnp.sum(parts_ref[...], axis=0)
    scale = lax.rsqrt(total / all_channels + epsilon)
    rows = tokens // tile
    for c in range(rows):
        here = pl.ds(c * tile, tile)
        rq[here, :] = jnp.broadcast_to(scale[c : c + 1, :], (tile, tile)).T
        rk[here, :] = jnp.broadcast_to(scale[rows + c : rows + c + 1, :], (tile, tile)).T

    def store(s):
        columns = pl.ds(pl.multiple_of(s * width, width), width)
        return pltpu.make_async_copy(out_buf.at[s], out_ref.at[:, columns], out_sems.at[s])

    def work(s, carry):
        at = first + s
        start = pl.multiple_of(head_at(at, kind_ref, heads) * size, size)
        gain_q = gq_ref[pl.ds(start, size)].reshape(1, size)
        gain_k = gk_ref[pl.ds(start, size)].reshape(1, size)
        normed_q = (staged_ref[at, :, 0:size].astype(F32) * rq[...] * gain_q).astype(BF)
        normed_k = (staged_ref[at, :, size : 2 * size].astype(F32) * rk[...] * gain_k).astype(BF)
        if joined:
            out_buf[s, :, 0:size] = normed_q
        else:
            qn_ref[:, pl.ds(pl.multiple_of(s * size, size), size)] = normed_q
        out_buf[s, :, width - 2 * size : width - size] = normed_k
        out_buf[s, :, width - size : width] = staged_ref[at, :, 2 * size : 3 * size]
        store(s).start()
        return carry

    lax.fori_loop(0, count, work, 0)

    def end(s, carry):
        store(s).wait()
        return carry

    lax.fori_loop(0, count, end, 0)


def pack(kind, parts, gain_q, gain_k, staged, after, first, count, joined, all_channels, tile):
    _, tokens, wide = staged.shape
    size = wide // 3
    width = (3 if joined else 2) * size
    out_shape = [jax.ShapeDtypeStruct((tokens, count * width), BF)]
    out_specs = [pl.BlockSpec(memory_space=pl.ANY)]
    if joined:
        out_shape = [pltpu.HBM((tokens, count * width), BF)]
    if not joined:
        out_shape.append(jax.ShapeDtypeStruct((tokens, count * size), BF))
        out_specs.append(pl.BlockSpec(memory_space=pltpu.VMEM))
    return pl.pallas_call(
        functools.partial(pack_kernel, all_channels, tile, first, count, joined),
        in_specs=[pl.BlockSpec(memory_space=pltpu.SMEM)]
        + [pl.BlockSpec(memory_space=pltpu.VMEM)] * 4
        + [pl.BlockSpec(memory_space=pl.ANY)] * len(after),
        out_specs=out_specs,
        out_shape=out_shape,
        scratch_shapes=[
            pltpu.VMEM((count, tokens, width), BF),
            pltpu.VMEM((tokens, size), F32),
            pltpu.VMEM((tokens, size), F32),
            pltpu.SemaphoreType.DMA((count,)),
        ],
        compiler_params=params(),
        cost_estimate=pl.CostEstimate(
            flops=4 * tokens * size * count,
            bytes_accessed=12 * tokens * size * count,
            transcendentals=0,
        ),
        name="pack_temporal" if joined else "pack_spatial",
    )(kind, parts, gain_q, gain_k, staged, *after)


def video_rows(frames, share):
    spans = []
    start = 0
    while start < frames:
        stop = min(frames, ((start + SHIFT) // VIDEO + 1) * VIDEO - SHIFT)
        spans.append((start * share, stop * share))
        start = stop
    return spans


def temporal_kernel(scale, count, share, x_ref, valid_ref, *rest):
    spans = video_rows(valid_ref.shape[1], share)
    out_ref, x_buf, out_buf, live_buf, *masks = rest[-6 - len(spans) : -2]
    in_sems, out_sems = rest[-2:]
    rows = x_ref.shape[0]
    frames = valid_ref.shape[1]
    size = out_buf.shape[2]

    def load(s):
        columns = pl.ds(pl.multiple_of(s * 3 * size, 3 * size), 3 * size)
        return pltpu.make_async_copy(x_ref.at[:, columns], x_buf.at[s], in_sems.at[s])

    def begin(s, carry):
        load(s).start()
        return carry

    lax.fori_loop(0, count, begin, 0)
    bits = share.bit_length() - 1
    live = jnp.where(valid_ref[...] > 0, 1.0, 0.0).astype(F32)
    owner = lax.broadcasted_iota(jnp.int32, (rows, frames), 0) >> bits
    hot = jnp.where(owner == lax.broadcasted_iota(jnp.int32, (rows, frames), 1), 1.0, 0.0)
    hot = hot.astype(BF)
    over = (((1,), (1,)), ((), ()))
    live_row = lax.dot_general(
        jnp.broadcast_to(live, (8, frames)).astype(BF), hot, over, preferred_element_type=F32
    )
    live_buf[...] = lax.dot_general(
        hot, jnp.broadcast_to(live, (size, frames)).astype(BF), over, preferred_element_type=F32
    )
    for (low, high), mask in zip(spans, masks):
        n = high - low
        at_row = lax.broadcasted_iota(jnp.int32, (n, n), 0)
        at_col = lax.broadcasted_iota(jnp.int32, (n, n), 1)
        same_token = ((at_row ^ at_col) & (share - 1)) == 0
        allowed = same_token & ((live_row[0:1, low:high] > 0.5) | (at_row == at_col))
        mask[...] = jnp.where(allowed, 0.0, LOW).astype(F32)

    def store(s):
        columns = pl.ds(pl.multiple_of(s * size, size), size)
        return pltpu.make_async_copy(out_buf.at[s], out_ref.at[:, columns], out_sems.at[s])

    for s in range(count):
        load(s).wait()
    for s in range(count):
        for (low, high), mask in zip(spans, masks):
            here = pl.ds(low, high - low)
            x = lax.dot_general(
                x_buf[s, here, 0:size],
                x_buf[s, here, size : 2 * size],
                over,
                preferred_element_type=F32,
            )
            x = x + mask[...]
            p = jnp.exp2((x - jnp.max(x, axis=1, keepdims=True)) * scale)
            total = jnp.sum(p, axis=1, keepdims=True)
            o = jnp.dot(
                p.astype(BF), x_buf[s, here, 2 * size : 3 * size], preferred_element_type=F32
            )
            out_buf[s, here, :] = (o / total * live_buf[here, :]).astype(BF)
        store(s).start()

    def end(s, carry):
        store(s).wait()
        return carry

    lax.fori_loop(0, count, end, 0)


def temporal(x, valid_row, after, count, share, size, scale):
    rows = x.shape[0]
    return pl.pallas_call(
        functools.partial(temporal_kernel, scale, count, share),
        in_specs=[
            pl.BlockSpec(memory_space=pl.ANY),
            pl.BlockSpec(memory_space=pltpu.VMEM),
        ]
        + [pl.BlockSpec(memory_space=pl.ANY)] * len(after),
        out_specs=pl.BlockSpec(memory_space=pl.ANY),
        out_shape=jax.ShapeDtypeStruct((rows, count * size), BF),
        scratch_shapes=[
            pltpu.VMEM((count, rows, 3 * size), BF),
            pltpu.VMEM((count, rows, size), BF),
            pltpu.VMEM((rows, size), F32),
            *[
                pltpu.VMEM((high - low, high - low), F32)
                for low, high in video_rows(valid_row.shape[1], share)
            ],
            pltpu.SemaphoreType.DMA((count,)),
            pltpu.SemaphoreType.DMA((count,)),
        ],
        compiler_params=params(),
        cost_estimate=pl.CostEstimate(
            flops=4 * rows * rows * size * count,
            bytes_accessed=8 * rows * size * count,
            transcendentals=rows * rows * count,
        ),
        name="temporal_heads",
    )(x, valid_row, *after)


def spatial_kernel(
    scale, tile, first, kind_ref, mask_ref, valid_ref, place_ref,
    q_ref, own_ref, before_ref, after_ref, out_ref
):
    heads = kind_ref.shape[0]
    head = head_at(first + pl.program_id(0), kind_ref, heads)
    tiles = own_ref.shape[0] // tile
    i = pl.program_id(1)
    frames = (before_ref, own_ref, after_ref)
    place = place_ref[0]
    last = valid_ref.shape[0] - 1
    near = [None, jnp.bool_(True), None]
    for o, there in ((0, jnp.maximum(place - 1, 0)), (2, jnp.minimum(place + 1, last))):
        same = ((there + SHIFT) // VIDEO == (place + SHIFT) // VIDEO) & (there != place)
        near[o] = same & (valid_ref[there] > 0)
    own_live = jnp.where(valid_ref[place] > 0, 1.0, 0.0).astype(F32)
    q = q_ref[...]
    pieces = []
    for o in range(3):
        s = lax.dot_general(
            q, frames[o][:, 0:128], (((1,), (1,)), ((), ())), preferred_element_type=F32
        )
        for j in range(tiles):
            ok = (mask_ref[head, i, o * tiles + j] > 0) & near[o]
            low = jnp.where(ok, 0.0, LOW).astype(F32)
            pieces.append(s[:, j * tile : (j + 1) * tile] + low)
    top = pieces[0]
    for x in pieces[1:]:
        top = jnp.maximum(top, x)
    top = jnp.max(top, axis=1, keepdims=True)
    pieces = [jnp.exp2((x - top) * scale) for x in pieces]
    total = pieces[0]
    for x in pieces[1:]:
        total = total + x
    total = jnp.sum(total, axis=1, keepdims=True)
    o_sum = None
    for o in range(3):
        p = jnp.concatenate([x.astype(BF) for x in pieces[o * tiles : (o + 1) * tiles]], axis=1)
        part = jnp.dot(p, frames[o][:, 128:256], preferred_element_type=F32)
        o_sum = part if o_sum is None else o_sum + part
    out_ref[...] = (o_sum / total * own_live).astype(BF)


def spatial(kind, mask, valid, place, q, own, before, after, first, count, channels, scale, tile):
    tokens = q.shape[0]
    heads = kind.shape[0]
    size = channels // heads

    def slot(i, j, *_):
        return (0, i)

    return pl.pallas_call(
        functools.partial(spatial_kernel, scale, tile, first),
        grid_spec=pltpu.PrefetchScalarGridSpec(
            num_scalar_prefetch=4,
            grid=(count, tokens // tile),
            in_specs=[pl.BlockSpec((tile, size), lambda i, j, *_: (j, i))]
            + [pl.BlockSpec((tokens, 2 * size), slot)] * 3,
            out_specs=pl.BlockSpec(
                (tile, size),
                lambda i, j, kind_ref, *_: (j, head_at(first + i, kind_ref, heads)),
            ),
        ),
        out_shape=jax.ShapeDtypeStruct((tokens, channels), BF),
        compiler_params=params(),
        cost_estimate=pl.CostEstimate(
            flops=12 * tokens * tokens * size * count,
            bytes_accessed=16 * tokens * size * count,
            transcendentals=3 * tokens * tokens * count,
        ),
        name="spatial_heads",
    )(kind, mask, valid, place, q, own, before, after)


def merge_kernel(count, blocks, kind_ref, base_ref, x_ref, out_ref, sems):
    heads = kind_ref.shape[0]
    size = out_ref.shape[1] // heads
    height = out_ref.shape[0] // blocks
    copies = []
    for s in range(count):
        start = pl.multiple_of(head_at(s, kind_ref, heads) * size, size)
        for i in range(blocks):
            rows = pl.ds(i * height, height)
            copy = pltpu.make_async_copy(
                x_ref.at[rows, pl.ds(s * size, size)],
                out_ref.at[rows, pl.ds(start, size)],
                sems.at[s * blocks + i],
            )
            copy.start()
            copies.append(copy)
    for copy in copies:
        copy.wait()


def merge(kind, base, x, count):
    return pl.pallas_call(
        functools.partial(merge_kernel, count, 4),
        in_specs=[pl.BlockSpec(memory_space=pltpu.SMEM)]
        + [pl.BlockSpec(memory_space=pltpu.HBM), pl.BlockSpec(memory_space=pl.ANY)],
        out_specs=pl.BlockSpec(memory_space=pltpu.HBM),
        out_shape=jax.ShapeDtypeStruct(base.shape, BF),
        scratch_shapes=[pltpu.SemaphoreType.DMA((4 * count,))],
        input_output_aliases={1: 0},
        compiler_params=params(),
        cost_estimate=pl.CostEstimate(flops=0, bytes_accessed=4 * x.size, transcendentals=0),
        name="merge_heads",
    )(kind, base, x)


def local(queries, keys, values, gain_q, gain_k, head_kind, tile_mask, frame_valid):
    heads = head_kind.shape[0]
    tokens, channels = queries.shape[1:]
    size = channels // heads
    tile = tokens // tile_mask.shape[1]
    frames = lax.axis_size("frames")
    blocks = lax.axis_size("heads")
    position = lax.axis_index("frames")
    scale = math.log2(math.e) / math.sqrt(size)
    share = tokens // frames
    q, k, v = queries[0], keys[0], values[0]

    odd = lax.axis_index("heads") % 2
    parts = local_sums(q, k, blocks, tile)
    staged, choice = stage(head_kind, odd[None], q, k, v)
    parts = lax.all_to_all(parts, "heads", split_axis=0, concat_axis=0, tiled=True)

    place = position[None]
    valid_row = frame_valid[None, :]
    up = [(i, i + 1) for i in range(frames - 1)]
    down = [(j, i) for i, j in up]

    def exchange(x):
        x = x.reshape(frames, share, x.shape[1])
        return lax.all_to_all(x, "frames", split_axis=0, concat_axis=0, tiled=True).reshape(
            tokens, x.shape[2]
        )

    def branch(count, late):
        rest = heads - count

        def run(staged, parts):
            args = (head_kind, parts, gain_q, gain_k, staged)

            def near():
                pair, near_q = pack(*args, (), count, rest, False, blocks * channels, tile)
                earlier = lax.ppermute(pair, "frames", up)
                later = lax.ppermute(pair, "frames", down)
                return near_q, pair, earlier, later

            def attend(near_q, pair, earlier, later):
                return spatial(
                    head_kind, tile_mask, frame_valid, place, near_q, pair, earlier, later,
                    count, rest, channels, scale, tile,
                )

            def send(*after):
                (sent,) = pack(*args, after, 0, count, True, blocks * channels, tile)
                return exchange(sent)

            if late == 0:
                mine = send()
                found = near()
                after = found[1:2]
            elif late == 1:
                found = near()
                mine = send(*found[2:])
                after = ()
            else:
                found = near()
                base = attend(*found)
                mine = send(base)
                after = ()
            told = temporal(mine, valid_row, after, count, share, size, scale)
            back = exchange(told)
            if late < 2:
                base = attend(*found)
            return merge(head_kind, base, back, count)

        return run

    branches = [branch(c, 0) for c in range(1, heads)]
    branches += [branch(c, 2) for c in range(3, heads)]
    out = lax.switch(choice[0], branches, staged, parts)
    return out[None]


def solution(mesh):
    placed = (
        P("frames", None, "heads"),
        P("frames", None, "heads"),
        P("frames", None, "heads"),
        P("heads"),
        P("heads"),
        P("heads"),
        P("heads", None, None),
        P(),
    )
    return jax.shard_map(
        local, mesh=mesh, in_specs=placed, out_specs=P("frames", None, "heads"), check_vma=False
    )
```
